512 devices in a mesh: row: 32 (over x, y), inner: 16 (over z, core).
Axes of the slice: x: 4, y: 8, z: 8, core: 2. Of those that a mesh axis runs over, the one named last changes fastest.
Arguments:
- h_blocks: bfloat16 [512, 32, 128, 128], P('row', 'inner'), may hold values from -0.09375 to 0.09375
- block_cols: int32 [512, 32], P('row', 'inner'), may hold values from 0 to 511, as said below
- panel_now: bfloat16 [65536, 192], P(('row', 'inner')), may hold values from -6 to 6
- panel_prev: bfloat16 [65536, 192], P(('row', 'inner')), may hold values from -6 to 6
- density: float32 [65536, 192], P(('row', 'inner')), may hold values from -6 to 6
- coeff: float32 [1], replicated, may hold values from 0.5 to 2
- cot_panel: bfloat16 [65536, 192], P(('row', 'inner')), may hold values from -2 to 2
- cot_density: bfloat16 [65536, 192], P(('row', 'inner')), may hold values from -2 to 2
Outputs:
- panel_next: bfloat16 [65536, 192], P(('row', 'inner'))
- density_next: float32 [65536, 192], P(('row', 'inner'))
- grad_now: float32 [65536, 192], P(('row', 'inner'))
- grad_h: bfloat16 [512, 32, 128, 128], P('row', 'inner')
The draws below stay inside these ranges and needn't reach their ends.
Inputs may be any that keep to these rules, and one draw needn't show every extreme that they name: `block_cols`: each block row b lists 32 distinct block columns, each within periodic distance 16 of b modulo 512.
All inputs are finite; a program needn't handle non-finite values.
Results may differ from the reference program's by a relative error of at most 0.022.
Values may be sent and summed in bfloat16 or wider, within the bound.
A program may use at most 64 MiB of HBM per device.

```python
import math
import jax
import jax.numpy as jnp
from jax import lax

BS = 128
CAP = 32
NV = 192
ROWS_DEV = 16
SLOTS_DEV = 2
NBLOCK = 512
NROWS = 65536


def draw_block_cols(key, part):
    key = jax.random.fold_in(key, 11)
    span = 2 * ROWS_DEV + 1
    scores = jax.random.randint(key, (NBLOCK, span), 0, 1 << 20)
    scores = scores * span + jnp.arange(span, dtype=jnp.int32)[None, :]
    _, ranking = lax.top_k(scores, CAP)
    offsets = ranking.astype(jnp.int32) - ROWS_DEV
    row_index = jnp.arange(NBLOCK, dtype=jnp.int32)[:, None]
    return ((row_index + offsets) % NBLOCK).astype(jnp.int32)


def block_levels(rng, shape, split, least, high):
    gain, own = 1.0, jax.random.fold_in(rng, 6)
    for dim, parts in split:
        draws = jnp.exp(jax.random.uniform(jax.random.fold_in(own, dim), (parts,), jnp.float32, least / len(split), high / len(split)))
        gain = gain * jnp.repeat(draws, shape[dim] // parts).reshape([-1 if axis == dim else 1 for axis in range(len(shape))])
    return gain


def centred(key, extent, scale, most, cuts=(), held_as=jnp.bfloat16):
    values = jax.random.normal(key, extent, jnp.float32) * scale
    if len(cuts) > 0:
        values = block_levels(key, extent, cuts, -0.22, 0.18) * values
    return jnp.clip(values, min=-most, max=most).astype(held_as)


def setup_inputs(seed: int = 0) -> dict:
    seeds = jax.random.split(jax.random.key(seed), 9)
    return {
        "h_blocks": centred(seeds[0], (NBLOCK, CAP, BS, BS), (CAP * BS) ** -0.5, 0.09375, ((0, 32), (1, 16))),
        "block_cols": draw_block_cols(jax.random.fold_in(seeds[8], 71), 0),
        "panel_now": centred(seeds[2], (NROWS, NV), 1.0, 6.0, ((0, 512),)),
        "panel_prev": centred(seeds[3], (NROWS, NV), 1.0, 6.0, ((0, 512),)),
        "density": centred(seeds[4], (NROWS, NV), 1.0, 6.0, ((0, 512),), jnp.float32),
        "coeff": jnp.clip(jnp.exp(jax.random.uniform(seeds[5], (1,), jnp.float32, math.log(0.5), math.log(2.0))), 0.5, 2.0),
        "cot_panel": centred(seeds[6], (NROWS, NV), 0.125, 2.0, ((0, 512),)),
        "cot_density": centred(seeds[7], (NROWS, NV), 0.125, 2.0, ((0, 512),)),
    }


def rounded(values):
    return lax.optimization_barrier(values.astype(jnp.bfloat16)).astype(jnp.float32)


def reference(h_blocks, block_cols, panel_now, panel_prev, density, coeff, cot_panel, cot_density):
    probe_count = panel_now.shape[1]
    scale = coeff[0]
    blocks_now = panel_now.reshape(NBLOCK, BS, probe_count).astype(jnp.float32)
    cot_total = (cot_panel.astype(jnp.float32) + scale * cot_density.astype(jnp.float32)).astype(jnp.bfloat16)
    cot_blocks = cot_total.reshape(NBLOCK, BS, probe_count).astype(jnp.float32)
    owner = jnp.arange(NBLOCK, dtype=jnp.int32) // ROWS_DEV
    groups_total = NBLOCK // ROWS_DEV
    product = jnp.zeros((NBLOCK, BS, probe_count), jnp.float32)
    back_total = jnp.zeros((3 * NBLOCK, BS, probe_count), jnp.float32)
    grad_slots = []
    for slot_group in range(CAP // SLOTS_DEV):
        partial_sum = jnp.zeros((NBLOCK, BS, probe_count), jnp.float32)
        returned = jnp.zeros((3 * NBLOCK, BS, probe_count), jnp.float32)
        for inner_slot in range(SLOTS_DEV):
            slot_index = slot_group * SLOTS_DEV + inner_slot
            columns = block_cols[:, slot_index].astype(jnp.int32)
            picked = blocks_now[columns]
            weights = h_blocks[:, slot_index].astype(jnp.float32)
            partial_sum = partial_sum + jnp.einsum("bij,bjn->bin", weights, picked)
            grad_slots.append(2.0 * jnp.einsum("bin,bjn->bij", cot_blocks, picked))
            back_term = jnp.einsum("bij,bin->bjn", weights, cot_blocks)
            offset = (owner - owner[columns]) % groups_total
            bucket = jnp.where(offset == 0, 1, jnp.where(offset == 1, 0, 2)).astype(jnp.int32)
            segment_ids = (columns * 3 + bucket).astype(jnp.int32)
            returned = returned + jax.ops.segment_sum(back_term, segment_ids, num_segments=3 * NBLOCK)
        product = product + rounded(partial_sum)
        back_total = back_total + rounded(returned)
    back = rounded(back_total).reshape(NBLOCK, 3, BS, probe_count)
    product = product.reshape(NROWS, probe_count)
    panel_next = (2.0 * product - panel_prev.astype(jnp.float32)).astype(jnp.bfloat16)
    density_next = density + scale * panel_next.astype(jnp.float32)
    grad_now = 2.0 * jnp.sum(back, axis=1).reshape(NROWS, probe_count)
    grad_h = jnp.stack(grad_slots, axis=1).astype(jnp.bfloat16)
    return (panel_next, density_next, grad_now, grad_h)
```

```python
import functools

import jax
import jax.numpy as jnp
from jax import lax
from jax.experimental import pallas as pl
from jax.experimental.pallas import tpu as pltpu
from jax.sharding import PartitionSpec as P

MESH = pl.DeviceIdType.MESH
F32 = jnp.float32
BF16 = jnp.bfloat16
NT = (((1,), (1,)), ((), ()))
NN = (((1,), (0,)), ((), ()))
TN = (((0,), (0,)), ((), ()))


def dot(a, b, dims):
    return lax.dot_general(a, b, dims, preferred_element_type=F32)


def kernel(
    rows, inner, meta, coeff, h, now, prev, dens, cotp, cotd,
    o_next, o_dens, o_grad, o_gh,
    hbuf, gbuf, v_now, v_prev, v_dens, v_cotp, v_cotd, v_next, v_dout, v_grad,
    win, cot, chain, tout, tsib, ysend, yrecv, pout, psib, rsend, rrecv,
    in_sem, out_sem, ring_s, ring_r, sib_s, sib_r, y_s, y_r, ysib_s, ysib_r,
    tsib_s, tsib_r, ty_s, ty_r, psib_s, psib_r, rs_s, rs_r,
):
    zs = inner // 2
    half = zs // 2
    nv, bs = win.shape[1:]
    lower, upper = pl.ds(0, nv // 2), pl.ds(nv // 2, nv // 2)
    part = (lower, upper)
    pairs = 2 * inner
    r = lax.axis_index("row")
    i = lax.axis_index("inner")
    z, c = i // 2, lax.rem(i, 2)
    o = 1 - c

    def at_z(step):
        return lax.rem(z + step + zs, zs)

    sibling = (r, 2 * z + o)
    along = ((r, 2 * at_z(1) + c), (r, 2 * at_z(-1) + c))
    row_up = (lax.rem(r + 1, rows), i)
    row_down = (lax.rem(r + rows - 1, rows), i)
    started = []

    def send(src, dst, s, v, device):
        copy = pltpu.make_async_remote_copy(
            src_ref=src, dst_ref=dst, send_sem=s, recv_sem=v,
            device_id=device, device_id_type=MESH,
        )
        copy.start()
        started.append(copy)
        return copy

    def pos(g, parity, zz):
        return (g * 2 + parity) * zs + zz

    loads = []
    for k, (src, dst) in enumerate(
        ((now, v_now), (cotp, v_cotp), (cotd, v_cotd), (h, hbuf), (prev, v_prev), (dens, v_dens))
    ):
        copy = pltpu.make_async_copy(src, dst, in_sem.at[k])
        copy.start()
        loads.append(copy)

    barrier = pltpu.get_barrier_semaphore()
    for device in (sibling, along[0], along[1], row_up, row_down):
        pl.semaphore_signal(barrier, inc=1, device_id=device, device_id_type=MESH)

    eye = (
        lax.broadcasted_iota(jnp.int32, (nv, nv), 0) == lax.broadcasted_iota(jnp.int32, (nv, nv), 1)
    ).astype(F32).astype(BF16)
    scale = coeff[0]
    loads[0].wait()
    win[pos(1, c, z)] = dot(eye, v_now[...], NT).astype(BF16)
    pl.semaphore_wait(barrier, 5)

    offs = [0]
    for k in range(1, half):
        offs += [-k, k]
    offs.append(half)

    held = (win, cot)
    base = (1, 0)
    ring = {}
    sib = {}
    ysent = {}

    def ring_send(a, way, step, off):
        ref = held[a].at[pos(base[a], c, at_z(off))]
        if step == half:
            ref = ref.at[part[way]]
        ring[a, way, step] = send(
            ref, ref, ring_s.at[a, way, step - 1], ring_r.at[a, way, step - 1], along[way]
        )

    def spread(a, j):
        zz = at_z(offs[j])
        src = held[a].at[pos(base[a], c, zz)]
        if a == 0:
            ysent[0, j] = send(src, win.at[pos(2, c, zz)], y_s.at[0, j], y_r.at[0, j], row_down)
            ysent[1, j] = send(src, win.at[pos(0, c, zz)], y_s.at[1, j], y_r.at[1, j], row_up)
        sib[a, j] = send(src, src, sib_s.at[a, j], sib_r.at[a, j], sibling)

    def own_out(a):
        ring_send(a, 0, 1, 0)
        ring_send(a, 1, 1, 0)
        spread(a, 0)

    own_out(0)
    loads[1].wait()
    loads[2].wait()
    total = (v_cotp[...].astype(F32) + scale * v_cotd[...].astype(F32)).astype(BF16)
    cot[pos(0, c, z)] = dot(eye, total, NT).astype(BF16)
    own_out(1)

    for k in range(1, half + 1):
        for a in range(2):
            for way in range(2):
                ring[a, way, k].wait_recv()
                if k < half:
                    ring_send(a, way, k + 1, -k if way == 0 else k)
                    spread(a, 2 * k - 1 + way)
            if k == half:
                spread(a, zs - 1)

    ysib = {}

    def y_forward(j):
        zz = at_z(offs[j])
        for way, g in ((0, 2), (1, 0)):
            ysent[way, j].wait_recv()
            ref = win.at[pos(g, c, zz)]
            ysib[way, j] = send(ref, ref, ysib_s.at[way, j], ysib_r.at[way, j], sibling)

    for j in range(half):
        y_forward(j)
    for j in range(zs):
        sib[1, j].wait_recv()
    loads[3].wait()

    chain[pairs] = jnp.zeros((nv, bs), F32)
    for b in range(inner):
        both = jnp.concatenate([hbuf[b, 0], hbuf[b, 1]], axis=1)
        back = dot(cot[pos(0, b % 2, b // 2)], both, NN)
        for s in range(2):
            p = 2 * b + s
            chain[p] = back[:, s * bs : (s + 1) * bs] + chain[meta[pairs + p]]

    def last(position):
        return chain[meta[2 * pairs + position]]

    tsent = {}
    for k, g in enumerate((0, 2, 1)):
        for zz in range(zs):
            tout[k, zz] = last(pos(g, o, zz)).astype(BF16)
        tsent[k] = send(tout.at[k], tsib.at[k], tsib_s.at[k], tsib_r.at[k], sibling)

    for j in range(half, zs):
        y_forward(j)

    far = [half]
    for k in range(half - 1, 0, -1):
        far += [k, -k]
    far.append(0)
    ty = {}
    tsent[0].wait_recv()
    tsent[1].wait_recv()
    for j, off in enumerate(far):
        zz = at_z(off)
        for k, g, device in ((0, 0, row_down), (1, 2, row_up)):
            ysend[k, zz] = (last(pos(g, c, zz)) + tsib[k, zz].astype(F32)).astype(BF16)
            ty[k, j] = send(
                ysend.at[k, zz], yrecv.at[k, zz], ty_s.at[k, j], ty_r.at[k, j], device
            )

    for j in range(zs):
        sib[0, j].wait_recv()
    for j in range(zs):
        for way in range(2):
            ysib[way, j].wait_recv()

    def picked(b):
        return jnp.concatenate([win[meta[2 * b]], win[meta[2 * b + 1]]], axis=1)

    def partial(b):
        both = jnp.concatenate([hbuf[b, 0], hbuf[b, 1]], axis=1)
        return dot(picked(b), both, NT)

    for b in range(inner):
        pout[pos(0, b % 2, b // 2)] = partial(b).astype(BF16)
    psent = send(
        pout.at[pl.ds(o * zs, zs)], psib, psib_s.at[0], psib_r.at[0], sibling
    )
    stores = []

    def grad_rows(first, count):
        for b in range(first, first + count):
            got = 2.0 * dot(cot[pos(0, b % 2, b // 2)], picked(b), TN)
            for s in range(2):
                gbuf[b, s] = got[:, s * bs : (s + 1) * bs].astype(BF16)
        span = pl.ds(first, count)
        copy = pltpu.make_async_copy(gbuf.at[span], o_gh.at[span], out_sem.at[len(stores)])
        copy.start()
        stores.append(copy)

    def term_here(off):
        j = far.index(off)
        for k in range(2):
            ty[k, j].wait_recv()
        zz = at_z(off)
        return (
            last(pos(1, c, zz)) + tsib[2, zz].astype(F32)
            + yrecv[0, zz].astype(F32) + yrecv[1, zz].astype(F32)
        )

    def product_here(off):
        zz = at_z(off)
        return pout[pos(0, c, zz)].astype(F32) + psib[zz].astype(F32)

    here = (product_here, term_here)
    rs = {}

    def rs_step(a, t):
        d = half + 1 - t
        shared = here[a](half) if t == 1 else None
        for way in range(2):
            out, got = rsend.at[a, way, t - 1], rrecv.at[a, way, t - 1]
            if t == 1:
                rows_here = part[way]
                start = way * (nv // 2)
                out[rows_here, :] = shared[start : start + nv // 2].astype(BF16)
                out, got = out.at[rows_here], got.at[rows_here]
            else:
                value = here[a](d if way == 0 else -d)
                rs[a, way, t - 1].wait_recv()
                if t == 2:
                    start = way * (nv // 2)
                    other = nv // 2 - start
                    out[part[way], :] = (
                        value[start : start + nv // 2]
                        + rrecv[a, way, 0, part[way], :].astype(F32)
                    ).astype(BF16)
                    out[part[1 - way], :] = value[other : other + nv // 2].astype(BF16)
                else:
                    out[...] = (value + rrecv[a, way, t - 2].astype(F32)).astype(BF16)
            rs[a, way, t] = send(
                out, got, rs_s.at[a, way, t - 1], rs_r.at[a, way, t - 1], along[way]
            )

    def finish(a):
        value = here[a](0)
        for way in range(2):
            rs[a, way, half].wait_recv()
            value = value + rrecv[a, way, half - 1].astype(F32)
        return value.T

    psent.wait_recv()
    tsent[2].wait_recv()
    chunk = inner // half
    for t in range(1, half + 1):
        rs_step(0, t)
        rs_step(1, t)
        grad_rows((t - 1) * chunk, chunk)

    loads[4].wait()
    loads[5].wait()
    nxt = (2.0 * finish(0) - v_prev[...].astype(F32)).astype(BF16)
    v_next[...] = nxt
    v_dout[...] = v_dens[...] + scale * nxt.astype(F32)
    for src, dst in ((v_next, o_next), (v_dout, o_dens)):
        copy = pltpu.make_async_copy(src, dst, out_sem.at[len(stores)])
        copy.start()
        stores.append(copy)
    v_grad[...] = 2.0 * finish(1)
    copy = pltpu.make_async_copy(v_grad, o_grad, out_sem.at[len(stores)])
    copy.start()
    stores.append(copy)
    for copy in stores:
        copy.wait()
    for copy in started:
        copy.wait_send()


def per_device(h, cols, now, prev, dens, coeff, cotp, cotd):
    inner, slots, bs, _ = h.shape
    nv = now.shape[1]
    rows = lax.axis_size("row")
    zs, half = inner // 2, inner // 4
    pairs = inner * slots
    first = lax.axis_index("row") * inner
    w = ((cols - first + inner) % (rows * inner)).reshape(pairs)
    g, ii = w // inner, w % inner
    where = (g * 2 + ii % 2) * zs + ii // 2
    q = jnp.arange(pairs, dtype=jnp.int32)
    targets = jnp.concatenate([where, jnp.arange(3 * inner, dtype=jnp.int32)])
    limit = jnp.concatenate([q, jnp.full((3 * inner,), pairs, jnp.int32)])
    hit = (targets[:, None] == where[None, :]) & (q[None, :] < limit[:, None])
    link = jnp.max(jnp.where(hit, q[None, :], -1), axis=1)
    link = jnp.where(link < 0, pairs, link)
    meta = jnp.concatenate([where, link])

    blk = (nv, bs)
    any_spec = pl.BlockSpec(memory_space=pl.ANY)
    smem = pl.BlockSpec(memory_space=pltpu.SMEM)
    vm = pltpu.VMEM
    sem = lambda *shape: pltpu.SemaphoreType.DMA(shape)
    scratch = [
        vm(h.shape, BF16), vm(h.shape, BF16),
        vm((bs, nv), BF16), vm((bs, nv), BF16), vm((bs, nv), F32), vm((bs, nv), BF16), vm((bs, nv), BF16),
        vm((bs, nv), BF16), vm((bs, nv), F32), vm((bs, nv), F32),
        vm((3 * inner, *blk), BF16), vm((inner, *blk), BF16), vm((pairs + 1, *blk), F32),
        vm((3, zs, *blk), BF16), vm((3, zs, *blk), BF16),
        vm((2, zs, *blk), BF16), vm((2, zs, *blk), BF16),
        vm((inner, *blk), BF16), vm((zs, *blk), BF16),
        vm((2, 2, half, *blk), BF16), vm((2, 2, half, *blk), BF16),
        sem(6), sem(half + 3), sem(2, 2, half), sem(2, 2, half), sem(2, zs), sem(2, zs),
        sem(2, zs), sem(2, zs), sem(2, zs), sem(2, zs),
        sem(3), sem(3), sem(2, zs), sem(2, zs), sem(1), sem(1), sem(2, 2, half), sem(2, 2, half),
    ]
    return pl.pallas_call(
        functools.partial(kernel, rows, inner),
        out_shape=(
            jax.ShapeDtypeStruct((bs, nv), BF16),
            jax.ShapeDtypeStruct((bs, nv), F32),
            jax.ShapeDtypeStruct((bs, nv), F32),
            jax.ShapeDtypeStruct(h.shape, BF16),
        ),
        in_specs=[smem, smem] + [any_spec] * 6,
        out_specs=(any_spec,) * 4,
        scratch_shapes=scratch,
        compiler_params=pltpu.CompilerParams(
            collective_id=0, has_side_effects=True, vmem_limit_bytes=40 * 1024 * 1024
        ),
        cost_estimate=pl.CostEstimate(
            flops=6 * pairs * bs * bs * nv, bytes_accessed=4 * h.size + 20 * bs * nv, transcendentals=0
        ),
    )(meta, coeff, h, now, prev, dens, cotp, cotd)


def solution(mesh):
    both = P(("row", "inner"), None)
    blocks = P("row", "inner", None, None)
    return jax.shard_map(
        per_device,
        mesh=mesh,
        in_specs=(blocks, P("row", "inner"), both, both, both, P(), both, both),
        out_specs=(both, both, both, blocks),
        check_vma=False,
    )
```

```python
import functools

import jax
import jax.numpy as jnp
from jax import lax
from jax.experimental import pallas as pl
from jax.experimental.pallas import tpu as pltpu
from jax.sharding import PartitionSpec as P

MESH = pl.DeviceIdType.MESH
F32 = jnp.float32
BF16 = jnp.bfloat16
NT = (((1,), (1,)), ((), ()))
NN = (((1,), (0,)), ((), ()))
TN = (((0,), (0,)), ((), ()))


def dot(a, b, dims):
    return lax.dot_general(a, b, dims, preferred_element_type=F32)


def kernel(
    rows, inner, meta, coeff, h, now, prev, dens, cotp, cotd,
    o_next, o_dens, o_grad, o_gh,
    hbuf, gbuf, v_now, v_prev, v_dens, v_cotp, v_cotd, v_next, v_dout, v_grad,
    win, cot, chain, tout, tsib, ysend, yrecv, pout, psib, rsend, rrecv,
    in_sem, out_sem, ring_s, ring_r, sib_s, sib_r, y_s, y_r, ysib_s, ysib_r,
    tsib_s, tsib_r, ty_s, ty_r, psib_s, psib_r, rs_s, rs_r,
):
    zs = inner // 2
    half = zs // 2
    nv, bs = win.shape[1:]
    lower, upper = pl.ds(0, nv // 2), pl.ds(nv // 2, nv // 2)
    part = (lower, upper)
    pairs = 2 * inner
    r = lax.axis_index("row")
    i = lax.axis_index("inner")
    z, c = i // 2, lax.rem(i, 2)
    o = 1 - c

    def at_z(step):
        return lax.rem(z + step + zs, zs)

    sibling = (r, 2 * z + o)
    along = ((r, 2 * at_z(1) + c), (r, 2 * at_z(-1) + c))
    row_up = (lax.rem(r + 1, rows), i)
    row_down = (lax.rem(r + rows - 1, rows), i)
    started = []

    def send(src, dst, s, v, device):
        copy = pltpu.make_async_remote_copy(
            src_ref=src, dst_ref=dst, send_sem=s, recv_sem=v,
            device_id=device, device_id_type=MESH,
        )
        copy.start()
        started.append(copy)
        return copy

    def pos(g, parity, zz):
        return (g * 2 + parity) * zs + zz

    loads = []
    for k, (src, dst) in enumerate(
        ((now, v_now), (cotp, v_cotp), (cotd, v_cotd), (h, hbuf), (prev, v_prev), (dens, v_dens))
    ):
        copy = pltpu.make_async_copy(src, dst, in_sem.at[k])
        copy.start()
        loads.append(copy)

    barrier = pltpu.get_barrier_semaphore()
    for device in (sibling, along[0], along[1], row_up, row_down):
        pl.semaphore_signal(barrier, inc=1, device_id=device, device_id_type=MESH)

    scale = coeff[0]
    loads[0].wait()
    win[pos(1, c, z)] = v_now[...]
    pl.semaphore_wait(barrier, 5)

    offs = [0]
    for k in range(1, half):
        offs += [-k, k]
    offs.append(half)

    held = (win, cot)
    base = (1, 0)
    ring = {}
    sib = {}
    ysent = {}

    def ring_send(a, way, step, off):
        ref = held[a].at[pos(base[a], c, at_z(off))]
        if step == half:
            ref = ref.at[part[way]]
        ring[a, way, step] = send(
            ref, ref, ring_s.at[a, way, step - 1], ring_r.at[a, way, step - 1], along[way]
        )

    def spread(a, j):
        zz = at_z(offs[j])
        src = held[a].at[pos(base[a], c, zz)]
        if a == 0:
            ysent[0, j] = send(src, win.at[pos(2, c, zz)], y_s.at[0, j], y_r.at[0, j], row_down)
            ysent[1, j] = send(src, win.at[pos(0, c, zz)], y_s.at[1, j], y_r.at[1, j], row_up)
        sib[a, j] = send(src, src, sib_s.at[a, j], sib_r.at[a, j], sibling)

    def own_out(a):
        ring_send(a, 0, 1, 0)
        ring_send(a, 1, 1, 0)
        spread(a, 0)

    own_out(0)
    loads[1].wait()
    loads[2].wait()
    total = (v_cotp[...].astype(F32) + scale * v_cotd[...].astype(F32)).astype(BF16)
    cot[pos(0, c, z)] = total
    own_out(1)

    for k in range(1, half + 1):
        for a in range(2):
            for way in range(2):
                ring[a, way, k].wait_recv()
                if k < half:
                    ring_send(a, way, k + 1, -k if way == 0 else k)
                    spread(a, 2 * k - 1 + way)
            if k == half:
                spread(a, zs - 1)

    ysib = {}

    def y_forward(j):
        zz = at_z(offs[j])
        for way, g in ((0, 2), (1, 0)):
            ysent[way, j].wait_recv()
            ref = win.at[pos(g, c, zz)]
            ysib[way, j] = send(ref, ref, ysib_s.at[way, j], ysib_r.at[way, j], sibling)

    for j in range(half):
        y_forward(j)
    for j in range(zs):
        sib[1, j].wait_recv()
    loads[3].wait()

    chain[pairs] = jnp.zeros((nv, bs), F32)
    for b in range(inner):
        both = jnp.concatenate([hbuf[b, 0], hbuf[b, 1]], axis=1)
        back = dot(cot[pos(0, b % 2, b // 2)], both, NN)
        for s in range(2):
            p = 2 * b + s
            chain[p] = back[:, s * bs : (s + 1) * bs] + chain[meta[pairs + p]]

    def last(position):
        return chain[meta[2 * pairs + position]]

    tsent = {}
    for k, g in enumerate((0, 2, 1)):
        for zz in range(zs):
            tout[k, zz] = last(pos(g, o, zz)).astype(BF16)
        tsent[k] = send(tout.at[k], tsib.at[k], tsib_s.at[k], tsib_r.at[k], sibling)

    for j in range(half, zs):
        y_forward(j)

    far = [half]
    for k in range(half - 1, 0, -1):
        far += [k, -k]
    far.append(0)
    ty = {}
    tsent[0].wait_recv()
    tsent[1].wait_recv()
    for j, off in enumerate(far):
        zz = at_z(off)
        for k, g, device in ((0, 0, row_down), (1, 2, row_up)):
            ysend[k, zz] = (last(pos(g, c, zz)) + tsib[k, zz].astype(F32)).astype(BF16)
            ty[k, j] = send(
                ysend.at[k, zz], yrecv.at[k, zz], ty_s.at[k, j], ty_r.at[k, j], device
            )

    for j in range(zs):
        sib[0, j].wait_recv()
    for j in range(zs):
        for way in range(2):
            ysib[way, j].wait_recv()

    def picked(b):
        return jnp.concatenate([win[meta[2 * b]], win[meta[2 * b + 1]]], axis=1)

    def partial(b):
        both = jnp.concatenate([hbuf[b, 0], hbuf[b, 1]], axis=1)
        return dot(picked(b), both, NT)

    for b in range(inner):
        pout[pos(0, b % 2, b // 2)] = partial(b).astype(BF16)
    psent = send(
        pout.at[pl.ds(o * zs, zs)], psib, psib_s.at[0], psib_r.at[0], sibling
    )
    stores = []

    def grad_rows(first, count):
        for b in range(first, first + count):
            got = 2.0 * dot(cot[pos(0, b % 2, b // 2)], picked(b), TN)
            for s in range(2):
                gbuf[b, s] = got[:, s * bs : (s + 1) * bs].astype(BF16)
        span = pl.ds(first, count)
        copy = pltpu.make_async_copy(gbuf.at[span], o_gh.at[span], out_sem.at[len(stores)])
        copy.start()
        stores.append(copy)

    def term_here(off):
        j = far.index(off)
        for k in range(2):
            ty[k, j].wait_recv()
        zz = at_z(off)
        return (
            last(pos(1, c, zz)) + tsib[2, zz].astype(F32)
            + yrecv[0, zz].astype(F32) + yrecv[1, zz].astype(F32)
        )

    def product_here(off):
        zz = at_z(off)
        return pout[pos(0, c, zz)].astype(F32) + psib[zz].astype(F32)

    here = (product_here, term_here)
    rs = {}

    def rs_step(a, t):
        d = half + 1 - t
        shared = here[a](half) if t == 1 else None
        for way in range(2):
            out, got = rsend.at[a, way, t - 1], rrecv.at[a, way, t - 1]
            if t == 1:
                rows_here = part[way]
                start = way * (nv // 2)
                out[rows_here, :] = shared[start : start + nv // 2].astype(BF16)
                out, got = out.at[rows_here], got.at[rows_here]
            else:
                value = here[a](d if way == 0 else -d)
                rs[a, way, t - 1].wait_recv()
                if t == 2:
                    start = way * (nv // 2)
                    other = nv // 2 - start
                    out[part[way], :] = (
                        value[start : start + nv // 2]
                        + rrecv[a, way, 0, part[way], :].astype(F32)
                    ).astype(BF16)
                    out[part[1 - way], :] = value[other : other + nv // 2].astype(BF16)
                else:
                    out[...] = (value + rrecv[a, way, t - 2].astype(F32)).astype(BF16)
            rs[a, way, t] = send(
                out, got, rs_s.at[a, way, t - 1], rs_r.at[a, way, t - 1], along[way]
            )

    def finish(a):
        value = here[a](0)
        for way in range(2):
            rs[a, way, half].wait_recv()
            value = value + rrecv[a, way, half - 1].astype(F32)
        return value

    psent.wait_recv()
    tsent[2].wait_recv()
    chunk = inner // half
    for t in range(1, half + 1):
        rs_step(0, t)
        rs_step(1, t)
        grad_rows((t - 1) * chunk, chunk)

    loads[4].wait()
    loads[5].wait()
    nxt = (2.0 * finish(0) - v_prev[...].astype(F32)).astype(BF16)
    v_next[...] = nxt
    v_dout[...] = v_dens[...] + scale * nxt.astype(F32)
    for src, dst in ((v_next, o_next), (v_dout, o_dens)):
        copy = pltpu.make_async_copy(src, dst, out_sem.at[len(stores)])
        copy.start()
        stores.append(copy)
    v_grad[...] = 2.0 * finish(1)
    copy = pltpu.make_async_copy(v_grad, o_grad, out_sem.at[len(stores)])
    copy.start()
    stores.append(copy)
    for copy in stores:
        copy.wait()
    for copy in started:
        copy.wait_send()


def per_device(h, cols, now, prev, dens, coeff, cotp, cotd):
    inner, slots, bs, _ = h.shape
    nv = now.shape[1]
    rows = lax.axis_size("row")
    zs, half = inner // 2, inner // 4
    pairs = inner * slots
    first = lax.axis_index("row") * inner
    w = ((cols - first + inner) % (rows * inner)).reshape(pairs)
    g, ii = w // inner, w % inner
    where = (g * 2 + ii % 2) * zs + ii // 2
    q = jnp.arange(pairs, dtype=jnp.int32)
    targets = jnp.concatenate([where, jnp.arange(3 * inner, dtype=jnp.int32)])
    limit = jnp.concatenate([q, jnp.full((3 * inner,), pairs, jnp.int32)])
    hit = (targets[:, None] == where[None, :]) & (q[None, :] < limit[:, None])
    link = jnp.max(jnp.where(hit, q[None, :], -1), axis=1)
    link = jnp.where(link < 0, pairs, link)
    meta = jnp.concatenate([where, link])

    blk = (nv, bs)
    any_spec = pl.BlockSpec(memory_space=pl.ANY)
    smem = pl.BlockSpec(memory_space=pltpu.SMEM)
    vm = pltpu.VMEM
    sem = lambda *shape: pltpu.SemaphoreType.DMA(shape)
    scratch = [
        vm(h.shape, BF16), vm(h.shape, BF16),
        vm(blk, BF16), vm(blk, BF16), vm(blk, F32), vm(blk, BF16), vm(blk, BF16),
        vm(blk, BF16), vm(blk, F32), vm(blk, F32),
        vm((3 * inner, *blk), BF16), vm((inner, *blk), BF16), vm((pairs + 1, *blk), F32),
        vm((3, zs, *blk), BF16), vm((3, zs, *blk), BF16),
        vm((2, zs, *blk), BF16), vm((2, zs, *blk), BF16),
        vm((inner, *blk), BF16), vm((zs, *blk), BF16),
        vm((2, 2, half, *blk), BF16), vm((2, 2, half, *blk), BF16),
        sem(6), sem(half + 3), sem(2, 2, half), sem(2, 2, half), sem(2, zs), sem(2, zs),
        sem(2, zs), sem(2, zs), sem(2, zs), sem(2, zs),
        sem(3), sem(3), sem(2, zs), sem(2, zs), sem(1), sem(1), sem(2, 2, half), sem(2, 2, half),
    ]
    out = pl.pallas_call(
        functools.partial(kernel, rows, inner),
        out_shape=(
            jax.ShapeDtypeStruct(blk, BF16),
            jax.ShapeDtypeStruct(blk, F32),
            jax.ShapeDtypeStruct(blk, F32),
            jax.ShapeDtypeStruct(h.shape, BF16),
        ),
        in_specs=[smem, smem] + [any_spec] * 6,
        out_specs=(any_spec,) * 4,
        scratch_shapes=scratch,
        compiler_params=pltpu.CompilerParams(
            collective_id=0, has_side_effects=True, vmem_limit_bytes=60 * 1024 * 1024
        ),
        cost_estimate=pl.CostEstimate(
            flops=6 * pairs * bs * bs * nv, bytes_accessed=4 * h.size + 20 * bs * nv, transcendentals=0
        ),
    )(meta, coeff, h, now.T, prev.T, dens.T, cotp.T, cotd.T)
    return (out[0].T, out[1].T, out[2].T, out[3])


def solution(mesh):
    both = P(("row", "inner"), None)
    blocks = P("row", "inner", None, None)
    return jax.shard_map(
        per_device,
        mesh=mesh,
        in_specs=(blocks, P("row", "inner"), both, both, both, P(), both, both),
        out_specs=(both, both, both, blocks),
        check_vma=False,
    )
```

```python
import functools

import jax
import jax.numpy as jnp
from jax import lax
from jax.experimental import pallas as pl
from jax.experimental.pallas import tpu as pltpu
from jax.sharding import PartitionSpec as P

MESH = pl.DeviceIdType.MESH
F32 = jnp.float32
BF16 = jnp.bfloat16
NT = (((1,), (1,)), ((), ()))
NN = (((1,), (0,)), ((), ()))
TN = (((0,), (0,)), ((), ()))


def dot(a, b, dims):
    return lax.dot_general(a, b, dims, preferred_element_type=F32)


def kernel(
    rows, inner, cols, coeff, h, now, prev, dens, cotp, cotd,
    o_next, o_dens, o_grad, o_gh,
    hbuf, gbuf, v_prev, v_dens, v_cotp, v_cotd, v_next, v_dout, v_grad,
    win, cot, chain, tout, tsib, ysend, yrecv, pout, psib, rsend, rrecv,
    where, link, last,
    in_sem, out_sem, ring_s, ring_r, sib_s, sib_r, y_s, y_r, ysib_s, ysib_r,
    tsib_s, tsib_r, ty_s, ty_r, psib_s, psib_r, rs_s, rs_r,
):
    zs = inner // 2
    half = zs // 2
    nv, bs = win.shape[1:]
    part = (pl.ds(0, nv // 2), pl.ds(nv // 2, nv // 2))
    pairs = 2 * inner
    total_blocks = rows * inner
    r = lax.axis_index("row")
    i = lax.axis_index("inner")
    z, c = i // 2, lax.rem(i, 2)
    o = 1 - c

    offs = [0]
    for k in range(1, half):
        offs += [-k, k]
    offs.append(half)

    def at_z(step):
        return lax.rem(z + step + zs, zs)

    sibling = (r, 2 * z + o)
    along = ((r, 2 * at_z(1) + c), (r, 2 * at_z(-1) + c))
    row_up = (lax.rem(r + 1, rows), i)
    row_down = (lax.rem(r + rows - 1, rows), i)
    started = []

    def send(src, dst, s, v, device):
        copy = pltpu.make_async_remote_copy(
            src_ref=src, dst_ref=dst, send_sem=s, recv_sem=v,
            device_id=device, device_id_type=MESH,
        )
        copy.start()
        started.append(copy)
        return copy

    def pos(g, parity, j=0):
        return (g * 2 + parity) * zs + j

    def run(g, parity, span):
        return pl.ds(pos(g, parity, span[0]), span[1])

    loads = []
    for k, (src, dst) in enumerate(
        ((now, win.at[pos(1, c)]), (cotp, v_cotp), (cotd, v_cotd), (h, hbuf), (prev, v_prev), (dens, v_dens))
    ):
        copy = pltpu.make_async_copy(src, dst, in_sem.at[k])
        copy.start()
        loads.append(copy)

    barrier = pltpu.get_barrier_semaphore()
    for device in (sibling, along[0], along[1], row_up, row_down):
        pl.semaphore_signal(barrier, inc=1, device_id=device, device_id_type=MESH)

    scale = coeff[0]
    loads[1].wait()
    loads[2].wait()
    cot[pos(0, c)] = (v_cotp[...].astype(F32) + scale * v_cotd[...].astype(F32)).astype(BF16)
    loads[0].wait()
    pl.semaphore_wait(barrier, 5)

    held = (win, cot)
    base = (1, 0)
    ring = {}
    sib = {}
    ysent = {}
    spans = [(0, 1)] + [(2 * k - 1, 2) for k in range(1, half)] + [(zs - 1, 1)]

    def ring_send(a, way, step, p):
        j = 0 if step == 1 else 2 * (step - 1) - 1 + way
        came = 0 if step == 1 else (zs - 1 if step > half else j)
        goes = zs - 1 if step == half else 2 * step - 1 + way
        src = held[a].at[pos(base[a], c, came)].at[part[p]]
        dst = held[a].at[pos(base[a], c, goes)].at[part[p]]
        ring[a, way, step, p] = send(
            src, dst, ring_s.at[a, way, step - 1, p], ring_r.at[a, way, step - 1, p], along[way]
        )

    def ring_out(a, step):
        for p in range(2):
            for way in range(2):
                if step < half or p == way:
                    ring_send(a, way, step, p)

    def ring_on(a, k):
        for p in range(2):
            for way in range(2):
                if k == half and p != way:
                    continue
                ring[a, way, k, p].wait_recv()
                if k < half - 1 or (k == half - 1 and p == way):
                    ring_send(a, way, k + 1, p)

    def to_sibling(a, n):
        ref = held[a].at[run(base[a], c, spans[n])]
        sib[a, n] = send(ref, ref, sib_s.at[a, n], sib_r.at[a, n], sibling)

    def to_rows(n):
        src = win.at[run(1, c, spans[n])]
        for way, g, device in ((0, 2, row_down), (1, 0, row_up)):
            ysent[way, n] = send(
                src, win.at[run(g, c, spans[n])], y_s.at[way, n], y_r.at[way, n], device
            )

    ring_out(1, 1)
    to_rows(0)
    to_sibling(1, 0)
    ring_out(0, 1)

    def block_of(j, parity):
        return 2 * at_z(offs[j]) + parity

    uses = []
    for begin, count in spans:
        for whose in range(2):
            uses += [(j, whose) for j in range(begin, begin + count)]
    parities = (c, o)

    first = r * inner
    for n, (j, whose) in enumerate(uses):
        b = block_of(j, parities[whose])
        for s in range(2):
            w = lax.rem(cols[s, b] - first + inner + total_blocks, total_blocks)
            w = jnp.minimum(w, 3 * inner - 1)
            g, ii = w // inner, lax.rem(w, inner)
            rel = lax.rem(ii // 2 - z + zs, zs)
            jj = jnp.where(rel <= half, jnp.minimum(2 * rel, zs - 1), 2 * (zs - rel) - 1)
            where[2 * n + s] = pos(g, lax.rem(ii, 2), jj)

    def find(value, stop):
        found = jnp.int32(pairs)
        for q in range(stop):
            found = jnp.where(where[q] == value, q, found)
        return found

    def find_links(n):
        for q in (2 * n, 2 * n + 1):
            link[q] = find(where[q], 2 * n)

    def find_last(begin, end):
        def body(k, carry):
            last[k] = find(k, pairs)
            return carry

        lax.fori_loop(begin, end, body, 0)

    chain[pairs] = jnp.zeros((nv, bs), F32)

    def hcat(b):
        return jnp.concatenate([hbuf[b, 0], hbuf[b, 1]], axis=1)

    def back(n, j, parity):
        find_links(n)
        got = dot(cot[pos(0, parity, j)], hcat(block_of(j, parity)), NN)
        for s in range(2):
            q = 2 * n + s
            chain[q] = got[:, s * bs : (s + 1) * bs] + chain[link[q]]

    def backs(n, whose):
        begin, count = spans[n]
        for j in range(begin, begin + count):
            back(uses.index((j, whose)), j, parities[whose])

    ysib = {}
    packs = ((0, half + 1), (half + 1, half - 1))

    def y_wait(n):
        for way in range(2):
            ysent[way, n].wait_recv()

    def pack_out(m):
        for way, g in ((0, 2), (1, 0)):
            ref = win.at[run(g, c, packs[m])]
            ysib[way, m] = send(ref, ref, ysib_s.at[way, m], ysib_r.at[way, m], sibling)
        ref = win.at[run(1, c, packs[m])]
        ysib[2, m] = send(ref, ref, ysib_s.at[2, m], ysib_r.at[2, m], sibling)

    share = 3 * inner // half
    loads[3].wait()
    for k in range(1, half + 1):
        ring_on(1, k)
        to_sibling(1, k)
        if k == 1:
            backs(0, 0)
        ring_on(0, k)
        to_rows(k)
        if k < half:
            find_last((k - 1) * share, k * share)
        sib[1, k - 1].wait_recv()
        backs(k - 1, 1)
        backs(k, 0)
    find_last((half - 1) * share, half * share)
    sib[1, half].wait_recv()
    backs(half, 1)

    def tail(g, parity, j):
        return chain[last[pos(g, parity, j)]]

    cuts = ((zs - 3, 3), (zs - 5, 2), (0, zs - 5))
    tsent = {}

    def tails_out(k, g, m):
        begin, count = cuts[m]
        for j in range(begin, begin + count):
            tout[k, j] = tail(g, o, j).astype(BF16)
        span = pl.ds(begin, count)
        tsent[k, m] = send(
            tout.at[k, span], tsib.at[k, span], tsib_s.at[k, m], tsib_r.at[k, m], sibling
        )

    for m in range(3):
        tails_out(0, 0, m)
        tails_out(1, 2, m)

    for n in range(half):
        y_wait(n)
        if n == half // 2:
            pack_out(0)

    ty = {}

    def to_owners(n):
        begin, count = spans[n]
        for k, g, device in ((0, 0, row_down), (1, 2, row_up)):
            for j in range(begin, begin + count):
                ysend[k, j] = (tail(g, c, j) + tsib[k, j].astype(F32)).astype(BF16)
            span = pl.ds(begin, count)
            ty[k, n] = send(
                ysend.at[k, span], yrecv.at[k, span], ty_s.at[k, n], ty_r.at[k, n], device
            )

    ready = {half: 0, half - 2: 1, half - 3: 2}
    for n in range(half, -1, -1):
        if n in ready:
            tsent[0, ready[n]].wait_recv()
            tsent[1, ready[n]].wait_recv()
        to_owners(n)
        if n == half - 1:
            y_wait(half)
            pack_out(1)
    for m in range(3):
        tails_out(2, 1, m)
    for m in range(2):
        for way in range(3):
            ysib[way, m].wait_recv()

    def picked(n):
        return jnp.concatenate([win[where[2 * n]], win[where[2 * n + 1]]], axis=1)

    def product(n, j, parity, k):
        pout[k, j] = dot(picked(n), hcat(block_of(j, parity)), NT).astype(BF16)

    psent = {}
    for m in range(3):
        begin, count = cuts[m]
        for j in range(begin, begin + count):
            product(uses.index((j, 1)), j, o, 1)
        span = pl.ds(begin, count)
        psent[m] = send(pout.at[1, span], psib.at[span], psib_s.at[m], psib_r.at[m], sibling)
    for j in range(zs - 1, -1, -1):
        product(uses.index((j, 0)), j, c, 0)

    stores = []

    def store(src, dst):
        copy = pltpu.make_async_copy(src, dst, out_sem.at[len(stores)])
        copy.start()
        stores.append(copy)

    def grad_rows(begin, count):
        for n in range(begin, begin + count):
            j, parity = uses[n][0], parities[uses[n][1]]
            b = block_of(j, parity)
            got = 2.0 * dot(cot[pos(0, parity, j)], picked(n), TN)
            for s in range(2):
                gbuf[b, s] = got[:, s * bs : (s + 1) * bs].astype(BF16)

    def half_of(ref, p):
        return ref[part[p], :].astype(F32)

    def product_here(j, p):
        return half_of(pout.at[0, j], p) + half_of(psib.at[j], p)

    def term_here(j, p):
        spot = chain.at[last[pos(1, c, j)]]
        return (
            spot[part[p], :] + half_of(tsib.at[2, j], p)
            + half_of(yrecv.at[0, j], p) + half_of(yrecv.at[1, j], p)
        )

    here = (product_here, term_here)
    rs = {}

    def rs_step(a, t):
        d = half + 1 - t
        if a == 1:
            for k in range(2):
                ty[k, d].wait_recv()
        for turn in range(2):
            for way in range(2):
                p = way if turn else 1 - way
                if t == 1 and p != way:
                    continue
                j = zs - 1 if t == 1 else 2 * d - 1 + (1 - way)
                value = here[a](j, p)
                if t > 2 or (t == 2 and p == way):
                    rs[a, way, t - 1, p].wait_recv()
                    value = value + half_of(rrecv.at[a, way, t - 2], p)
                out = rsend.at[a, way, t - 1]
                out[part[p], :] = value.astype(BF16)
                rs[a, way, t, p] = send(
                    out.at[part[p]], rrecv.at[a, way, t - 1].at[part[p]],
                    rs_s.at[a, way, t - 1, p], rs_r.at[a, way, t - 1, p], along[way],
                )

    def finish(a, p):
        value = here[a](0, p)
        for way in range(2):
            rs[a, way, half, p].wait_recv()
            value = value + half_of(rrecv.at[a, way, half - 1], p)
        return value

    pneed = {1: 0, 3: 1, 4: 2}
    chunk = inner // half
    for t in range(1, half + 1):
        if t in pneed:
            psent[pneed[t]].wait_recv()
            tsent[2, pneed[t]].wait_recv()
        rs_step(0, t)
        rs_step(1, t)
        grad_rows((t - 1) * chunk, chunk)
    store(gbuf, o_gh)

    loads[4].wait()
    loads[5].wait()
    for p in range(2):
        nxt = (2.0 * finish(0, p) - half_of(v_prev, p)).astype(BF16)
        v_next[part[p], :] = nxt
        v_dout[part[p], :] = v_dens[part[p], :] + scale * nxt.astype(F32)
    store(v_next, o_next)
    store(v_dout, o_dens)
    for k in range(2):
        ty[k, 0].wait_recv()
    for p in range(2):
        v_grad[part[p], :] = 2.0 * finish(1, p)
    store(v_grad, o_grad)
    for copy in stores:
        copy.wait()
    for copy in started:
        copy.wait_send()


def per_device(h, cols, now, prev, dens, coeff, cotp, cotd):
    inner, slots, bs, _ = h.shape
    nv = now.shape[1]
    rows = lax.axis_size("row")
    zs, half = inner // 2, inner // 4
    pairs = inner * slots
    blk = (nv, bs)
    any_spec = pl.BlockSpec(memory_space=pl.ANY)
    hbm = pl.BlockSpec(memory_space=pltpu.HBM)
    smem = pl.BlockSpec(memory_space=pltpu.SMEM)
    vm = pltpu.VMEM
    sem = lambda *shape: pltpu.SemaphoreType.DMA(shape)
    scratch = [
        vm(h.shape, BF16), vm(h.shape, BF16),
        vm(blk, BF16), vm(blk, F32), vm(blk, BF16), vm(blk, BF16),
        vm(blk, BF16), vm(blk, F32), vm(blk, F32),
        vm((3 * inner, *blk), BF16), vm((inner, *blk), BF16), vm((pairs + 1, *blk), F32),
        vm((3, zs, *blk), BF16), vm((3, zs, *blk), BF16),
        vm((2, zs, *blk), BF16), vm((2, zs, *blk), BF16),
        vm((2, zs, *blk), BF16), vm((zs, *blk), BF16),
        vm((2, 2, half, *blk), BF16), vm((2, 2, half, *blk), BF16),
        pltpu.SMEM((pairs,), jnp.int32), pltpu.SMEM((pairs,), jnp.int32),
        pltpu.SMEM((3 * inner,), jnp.int32),
        sem(6), sem(4), sem(2, 2, half, 2), sem(2, 2, half, 2), sem(2, half + 1), sem(2, half + 1),
        sem(2, half + 1), sem(2, half + 1), sem(3, 2), sem(3, 2),
        sem(3, 3), sem(3, 3), sem(2, half + 1), sem(2, half + 1), sem(3), sem(3),
        sem(2, 2, half, 2), sem(2, 2, half, 2),
    ]
    out = pl.pallas_call(
        functools.partial(kernel, rows, inner),
        out_shape=(
            jax.ShapeDtypeStruct(blk, BF16),
            jax.ShapeDtypeStruct(blk, F32),
            jax.ShapeDtypeStruct(blk, F32),
            jax.ShapeDtypeStruct(h.shape, BF16),
        ),
        in_specs=[smem, smem] + [hbm] * 6,
        out_specs=(any_spec,) * 4,
        scratch_shapes=scratch,
        compiler_params=pltpu.CompilerParams(
            collective_id=0, has_side_effects=True, vmem_limit_bytes=40 * 1024 * 1024
        ),
        cost_estimate=pl.CostEstimate(
            flops=6 * pairs * bs * bs * nv, bytes_accessed=4 * h.size + 20 * bs * nv, transcendentals=0
        ),
    )(pltpu.with_memory_space_constraint(cols.T, pltpu.HBM), coeff, *[pltpu.with_memory_space_constraint(x, pltpu.HBM) for x in (h, now.T, prev.T, dens.T, cotp.T, cotd.T)])
    return (out[0].T, out[1].T, out[2].T, out[3])


def solution(mesh):
    both = P(("row", "inner"), None)
    blocks = P("row", "inner", None, None)
    return jax.shard_map(
        per_device,
        mesh=mesh,
        in_specs=(blocks, P("row", "inner"), both, both, both, P(), both, both),
        out_specs=(both, both, both, blocks),
        check_vma=False,
    )
```

```python
import functools

import jax
import jax.numpy as jnp
from jax import lax
from jax.experimental import pallas as pl
from jax.experimental.pallas import tpu as pltpu
from jax.sharding import PartitionSpec as P

MESH = pl.DeviceIdType.MESH
F32 = jnp.float32
BF16 = jnp.bfloat16
NT = (((1,), (1,)), ((), ()))
NN = (((1,), (0,)), ((), ()))
TN = (((0,), (0,)), ((), ()))


def dot(a, b, dims):
    return lax.dot_general(a, b, dims, preferred_element_type=F32)


def kernel(
    rows, inner, cols, coeff, h, now, prev, dens, cotp, cotd,
    o_next, o_dens, o_grad, o_gh,
    hbuf, v_prev, v_dens, v_cotp, v_cotd,
    win, cot, chain, tout, tsib, ysend, yrecv, pout, psib, rsend, rrecv,
    where, link, v_links,
    in_sem, ring_s, ring_r, sib_s, sib_r, y_s, y_r, ysib_s, ysib_r,
    tsib_s, tsib_r, ty_s, ty_r, psib_s, psib_r, rs_s, rs_r,
):
    zs = inner // 2
    half = zs // 2
    nv, bs = win.shape[1:]
    part = (pl.ds(0, nv // 2), pl.ds(nv // 2, nv // 2))
    pairs = 2 * inner
    total_blocks = rows * inner
    r = lax.axis_index("row")
    i = lax.axis_index("inner")
    z, c = i // 2, lax.rem(i, 2)
    o = 1 - c

    offs = [0]
    for k in range(1, half):
        offs += [-k, k]
    offs.append(half)

    def at_z(step):
        return lax.rem(z + step + zs, zs)

    sibling = (r, 2 * z + o)
    along = ((r, 2 * at_z(1) + c), (r, 2 * at_z(-1) + c))
    beyond = ((r, 2 * at_z(2) + c), (r, 2 * at_z(-2) + c))
    row_up = (lax.rem(r + 1, rows), i)
    row_down = (lax.rem(r + rows - 1, rows), i)
    started = []

    def send(src, dst, s, v, device):
        copy = pltpu.make_async_remote_copy(
            src_ref=src, dst_ref=dst, send_sem=s, recv_sem=v,
            device_id=device, device_id_type=MESH,
        )
        copy.start()
        started.append(copy)
        return copy

    def pos(g, parity, j=0):
        return (g * 2 + parity) * zs + j

    def run(g, parity, span):
        return pl.ds(pos(g, parity, span[0]), span[1])

    loads = []
    for k, (src, dst) in enumerate(
        ((now, win.at[pos(1, c)]), (cotp, v_cotp), (cotd, v_cotd), (h, hbuf), (prev, v_prev), (dens, v_dens))
    ):
        copy = pltpu.make_async_copy(src, dst, in_sem.at[k])
        copy.start()
        loads.append(copy)

    barrier = pltpu.get_barrier_semaphore()
    for device in (sibling, *along, *beyond, row_up, row_down):
        pl.semaphore_signal(barrier, inc=1, device_id=device, device_id_type=MESH)

    scale = coeff[0]
    loads[1].wait()
    loads[2].wait()
    cot[pos(0, c)] = (v_cotp[...].astype(F32) + scale * v_cotd[...].astype(F32)).astype(BF16)
    loads[0].wait()
    pl.semaphore_wait(barrier, 7)

    held = (win, cot)
    base = (1, 0)
    ring = {}
    sib = {}
    ysent = {}
    spans = [(0, 1)] + [(2 * k - 1, 2) for k in range(1, half)] + [(zs - 1, 1)]

    def place(a, j):
        return held[a].at[pos(base[a], c, j)]

    def pass_on(a, way, kind):
        came, goes, device = (
            (0, 3, beyond), (0, 1, along), (3, 5, along), (3, zs - 1, beyond)
        )[kind]
        src = place(a, came + way if came else 0)
        dst = place(a, goes + way if kind < 3 else goes)
        if kind == 3:
            src, dst = src.at[part[way]], dst.at[part[way]]
        ring[a, way, kind] = send(
            src, dst, ring_s.at[a, way, kind], ring_r.at[a, way, kind], device[way]
        )

    def own_out(a, kind):
        for way in range(2):
            pass_on(a, way, kind)

    def came_in(a, kind):
        for way in range(2):
            ring[a, way, kind].wait_recv()
            if kind == 0:
                pass_on(a, way, 2)
                pass_on(a, way, 3)

    def to_sibling(a, n):
        ref = held[a].at[run(base[a], c, spans[n])]
        sib[a, n] = send(ref, ref, sib_s.at[a, n], sib_r.at[a, n], sibling)

    def to_rows(n):
        src = win.at[run(1, c, spans[n])]
        for way, g, device in ((0, 2, row_down), (1, 0, row_up)):
            ysent[way, n] = send(
                src, win.at[run(g, c, spans[n])], y_s.at[way, n], y_r.at[way, n], device
            )

    own_out(1, 0)
    own_out(1, 1)
    to_sibling(1, 0)
    to_rows(0)
    own_out(0, 0)

    def block_of(j, parity):
        return 2 * at_z(offs[j]) + parity

    uses = []
    for n, whose in (
        (0, 0), (0, 1), (2, 0), (2, 1), (1, 0), (1, 1), (3, 0), (4, 0), (3, 1), (4, 1)
    ):
        begin, count = spans[n]
        uses += [(j, whose) for j in range(begin, begin + count)]
    parities = (c, o)

    first = r * inner
    listed = []
    for n, (j, whose) in enumerate(uses):
        b = block_of(j, parities[whose])
        for s in range(2):
            w = lax.rem(cols[s, b] - first + inner + total_blocks, total_blocks)
            w = jnp.minimum(w, 3 * inner - 1)
            g, ii = w // inner, lax.rem(w, inner)
            rel = lax.rem(ii // 2 - z + zs, zs)
            jj = jnp.where(rel <= half, jnp.minimum(2 * rel, zs - 1), 2 * (zs - rel) - 1)
            listed.append(pos(g, lax.rem(ii, 2), jj))
            where[2 * n + s] = listed[-1]

    lane = lax.broadcasted_iota(jnp.int32, (1, 128), 1)
    ends = jnp.full((1, 128), pairs, jnp.int32)
    spots = jnp.full((1, 128), -1, jnp.int32)
    before = jnp.full((1, 128), pairs, jnp.int32)
    for q in range(pairs):
        ends = jnp.where(lane == listed[q], q, ends)
        spots = jnp.where(lane == q, listed[q], spots)
    for q in range(pairs):
        before = jnp.where((spots == listed[q]) & (lane > q), q, before)
    v_links[0:1, :] = ends
    v_links[1:2, :] = before
    links = pltpu.make_async_copy(v_links, link, in_sem.at[6])
    links.start()

    chain[pairs] = jnp.zeros((nv, bs), F32)

    def hcat(b):
        return jnp.concatenate([hbuf[b, 0], hbuf[b, 1]], axis=1)

    def back(n, j, parity):
        got = dot(cot[pos(0, parity, j)], hcat(block_of(j, parity)), NN)
        for s in range(2):
            q = 2 * n + s
            chain[q] = got[:, s * bs : (s + 1) * bs] + chain[link[1, q]]

    def backs(n, whose):
        begin, count = spans[n]
        for j in range(begin, begin + count):
            back(uses.index((j, whose)), j, parities[whose])

    ysib = {}
    packs = ((0, half + 1), (half + 1, half - 1))

    def y_wait(n):
        for way in range(2):
            ysent[way, n].wait_recv()

    def pack_out(m):
        for way, g in ((0, 2), (1, 0)):
            ref = win.at[run(g, c, packs[m])]
            ysib[way, m] = send(ref, ref, ysib_s.at[way, m], ysib_r.at[way, m], sibling)
        ref = win.at[run(1, c, packs[m])]
        ysib[2, m] = send(ref, ref, ysib_s.at[2, m], ysib_r.at[2, m], sibling)

    def backs_there(n):
        sib[1, n].wait_recv()
        backs(n, 1)

    came_in(1, 0)
    to_sibling(1, 2)
    own_out(0, 1)
    loads[3].wait()
    links.wait()
    backs(0, 0)
    backs_there(0)
    came_in(1, 1)
    to_sibling(1, 1)
    backs(2, 0)
    came_in(0, 0)
    to_rows(2)
    backs_there(2)
    backs(1, 0)
    came_in(1, 2)
    to_sibling(1, 3)
    came_in(1, 3)
    to_sibling(1, 4)
    came_in(0, 1)
    to_rows(1)
    backs_there(1)
    backs(3, 0)
    backs(4, 0)
    came_in(0, 2)
    to_rows(3)
    came_in(0, 3)
    to_rows(4)
    backs_there(3)
    backs_there(4)

    def tail(g, parity, j):
        return chain[link[0, pos(g, parity, j)]]

    cuts = ((zs - 3, 3), (zs - 5, 2), (0, zs - 5))
    tsent = {}

    def tails_out(k, g, m):
        begin, count = cuts[m]
        for j in range(begin, begin + count):
            tout[k, j] = tail(g, o, j).astype(BF16)
        span = pl.ds(begin, count)
        tsent[k, m] = send(
            tout.at[k, span], tsib.at[k, span], tsib_s.at[k, m], tsib_r.at[k, m], sibling
        )

    for m in range(3):
        tails_out(0, 0, m)
        tails_out(1, 2, m)

    for n in (0, 2, 1):
        y_wait(n)
    pack_out(0)
    ty = {}

    def to_owners(n):
        begin, count = spans[n]
        for k, g, device in ((0, 0, row_down), (1, 2, row_up)):
            for j in range(begin, begin + count):
                ysend[k, j] = (tail(g, c, j) + tsib[k, j].astype(F32)).astype(BF16)
            span = pl.ds(begin, count)
            ty[k, n] = send(
                ysend.at[k, span], yrecv.at[k, span], ty_s.at[k, n], ty_r.at[k, n], device
            )

    ready = {half: 0, half - 2: 1, half - 3: 2}
    for n in range(half, -1, -1):
        if n in ready:
            tsent[0, ready[n]].wait_recv()
            tsent[1, ready[n]].wait_recv()
        to_owners(n)
    y_wait(3)
    y_wait(4)
    pack_out(1)
    for m in range(3):
        tails_out(2, 1, m)
    for m in range(2):
        for way in range(3):
            ysib[way, m].wait_recv()

    def picked(n):
        return jnp.concatenate([win[where[2 * n]], win[where[2 * n + 1]]], axis=1)

    def product(n, j, parity, k):
        pout[k, j] = dot(picked(n), hcat(block_of(j, parity)), NT).astype(BF16)

    psent = {}
    for m in range(3):
        begin, count = cuts[m]
        for j in range(begin, begin + count):
            product(uses.index((j, 1)), j, o, 1)
        span = pl.ds(begin, count)
        psent[m] = send(pout.at[1, span], psib.at[span], psib_s.at[m], psib_r.at[m], sibling)
    for j in range(zs - 1, -1, -1):
        product(uses.index((j, 0)), j, c, 0)

    def grad_rows(begin, count):
        for n in range(begin, begin + count):
            j, parity = uses[n][0], parities[uses[n][1]]
            b = block_of(j, parity)
            got = 2.0 * dot(cot[pos(0, parity, j)], picked(n), TN)
            for s in range(2):
                o_gh[b, s] = got[:, s * bs : (s + 1) * bs].astype(BF16)

    def product_here(j):
        return pout[0, j].astype(F32) + psib[j].astype(F32)

    def term_here(j):
        return (
            tail(1, c, j) + tsib[2, j].astype(F32)
            + yrecv[0, j].astype(F32) + yrecv[1, j].astype(F32)
        )

    here = (product_here, term_here)
    rs = {}

    def rs_send(a, way, kind, value, device, span=None):
        out, got = rsend.at[a, way, kind], rrecv.at[a, way, kind]
        if span is not None:
            out, got = out.at[span], got.at[span]
        out[...] = value.astype(BF16)
        rs[a, way, kind] = send(
            out, got, rs_s.at[a, way, kind], rs_r.at[a, way, kind], device[way]
        )

    def rs_far(a):
        far = here[a](zs - 1)
        for way in range(2):
            start = way * (nv // 2)
            rs_send(a, way, 1, far[start : start + nv // 2], beyond, part[way])
        for way in range(2):
            rs_send(a, way, 0, here[a](6 - way), along)

    def rs_middle(a):
        for way in range(2):
            value = here[a](4 - way)
            rs[a, way, 1].wait_recv()
            rs[a, way, 0].wait_recv()
            more = rrecv[a, way, 1, part[way], :].astype(F32)
            blank = jnp.zeros_like(more)
            more = jnp.concatenate((more, blank) if way == 0 else (blank, more), axis=0)
            value = value + rrecv[a, way, 0].astype(F32) + more
            rs_send(a, way, 2, value, beyond)

    def rs_near(a):
        for way in range(2):
            rs_send(a, way, 3, here[a](2 - way), along)

    def finish(a):
        value = here[a](0)
        for way in range(2):
            for kind in (3, 2):
                rs[a, way, kind].wait_recv()
                value = value + rrecv[a, way, kind].astype(F32)
        return value

    def y_here(n):
        for k in range(2):
            ty[k, n].wait_recv()

    chunk = inner // 4
    psent[0].wait_recv()
    rs_far(0)
    grad_rows(0, chunk)
    y_here(4)
    y_here(3)
    tsent[2, 0].wait_recv()
    rs_far(1)
    psent[1].wait_recv()
    rs_middle(0)
    psent[2].wait_recv()
    rs_near(0)
    grad_rows(chunk, chunk)
    y_here(2)
    tsent[2, 1].wait_recv()
    rs_middle(1)
    y_here(1)
    tsent[2, 2].wait_recv()
    rs_near(1)
    grad_rows(2 * chunk, 2 * chunk)

    loads[4].wait()
    loads[5].wait()
    nxt = (2.0 * finish(0) - v_prev[...].astype(F32)).astype(BF16)
    o_next[...] = nxt
    o_dens[...] = v_dens[...] + scale * nxt.astype(F32)
    y_here(0)
    o_grad[...] = 2.0 * finish(1)
    for copy in started:
        copy.wait_send()


def write_out(*refs):
    count = len(refs) // 2
    sems = refs[-1]
    copies = [
        pltpu.make_async_copy(refs[k], refs[count + k], sems.at[k]) for k in range(count)
    ]
    for copy in copies:
        copy.start()
    for copy in copies:
        copy.wait()


def per_device(h, cols, now, prev, dens, coeff, cotp, cotd):
    inner, slots, bs, _ = h.shape
    nv = now.shape[1]
    rows = lax.axis_size("row")
    zs, half = inner // 2, inner // 4
    pairs = inner * slots
    blk = (nv, bs)
    any_spec = pl.BlockSpec(memory_space=pl.ANY)
    hbm = pl.BlockSpec(memory_space=pltpu.HBM)
    vmem = pl.BlockSpec(memory_space=pltpu.VMEM)
    smem = pl.BlockSpec(memory_space=pltpu.SMEM)
    vm = pltpu.VMEM
    sem = lambda *shape: pltpu.SemaphoreType.DMA(shape)
    scratch = [
        vm(h.shape, BF16),
        vm(blk, BF16), vm(blk, F32), vm(blk, BF16), vm(blk, BF16),
        vm((3 * inner, *blk), BF16), vm((inner, *blk), BF16), vm((pairs + 1, *blk), F32),
        vm((3, zs, *blk), BF16), vm((3, zs, *blk), BF16),
        vm((2, zs, *blk), BF16), vm((2, zs, *blk), BF16),
        vm((2, zs, *blk), BF16), vm((zs, *blk), BF16),
        vm((2, 2, half, *blk), BF16), vm((2, 2, half, *blk), BF16),
        pltpu.SMEM((pairs,), jnp.int32), pltpu.SMEM((2, 128), jnp.int32),
        vm((2, 128), jnp.int32),
        sem(7), sem(2, 2, 4), sem(2, 2, 4), sem(2, half + 1), sem(2, half + 1),
        sem(2, half + 1), sem(2, half + 1), sem(3, 2), sem(3, 2),
        sem(3, 3), sem(3, 3), sem(2, half + 1), sem(2, half + 1), sem(3), sem(3),
        sem(2, 2, 4), sem(2, 2, 4),
    ]
    out = pl.pallas_call(
        functools.partial(kernel, rows, inner),
        out_shape=(
            jax.ShapeDtypeStruct(blk, BF16),
            jax.ShapeDtypeStruct(blk, F32),
            jax.ShapeDtypeStruct(blk, F32),
            jax.ShapeDtypeStruct(h.shape, BF16),
        ),
        in_specs=[smem, smem] + [hbm] * 6,
        out_specs=(vmem,) * 4,
        scratch_shapes=scratch,
        compiler_params=pltpu.CompilerParams(
            collective_id=0, has_side_effects=True, vmem_limit_bytes=40 * 1024 * 1024
        ),
        cost_estimate=pl.CostEstimate(
            flops=6 * pairs * bs * bs * nv, bytes_accessed=4 * h.size + 20 * bs * nv, transcendentals=0
        ),
    )(pltpu.with_memory_space_constraint(cols.T, pltpu.HBM), coeff, *[pltpu.with_memory_space_constraint(x, pltpu.HBM) for x in (h, now.T, prev.T, dens.T, cotp.T, cotd.T)])
    out = pl.pallas_call(
        write_out,
        out_shape=tuple(jax.ShapeDtypeStruct(x.shape, x.dtype) for x in out),
        in_specs=[any_spec] * 4,
        out_specs=(any_spec,) * 4,
        scratch_shapes=[sem(4)],
        compiler_params=pltpu.CompilerParams(vmem_limit_bytes=1024 * 1024),
    )(*out)
    return (out[0].T, out[1].T, out[2].T, out[3])


def solution(mesh):
    both = P(("row", "inner"), None)
    blocks = P("row", "inner", None, None)
    return jax.shard_map(
        per_device,
        mesh=mesh,
        in_specs=(blocks, P("row", "inner"), both, both, both, P(), both, both),
        out_specs=(both, both, both, blocks),
        check_vma=False,
    )
```

```python
import functools

import jax
import jax.numpy as jnp
from jax import lax
from jax.experimental import pallas as pl
from jax.experimental.pallas import tpu as pltpu
from jax.sharding import PartitionSpec as P

MESH = pl.DeviceIdType.MESH
F32 = jnp.float32
BF16 = jnp.bfloat16
NT = (((1,), (1,)), ((), ()))
NN = (((1,), (0,)), ((), ()))
TN = (((0,), (0,)), ((), ()))


def dot(a, b, dims):
    return lax.dot_general(a, b, dims, preferred_element_type=F32)


def kernel(
    rows, inner, cols, coeff, h, now, prev, dens, cotp, cotd,
    o_next, o_dens, o_grad, o_gh,
    hbuf, v_prev, v_dens, v_cotp, v_cotd,
    win, cot, chain, tout, tsib, ysend, yrecv, pout, psib, rsend, rrecv,
    where, link, v_links,
    in_sem, ring_s, ring_r, sib_s, sib_r, y_s, y_r, ysib_s, ysib_r,
    tsib_s, tsib_r, ty_s, ty_r, psib_s, psib_r, rs_s, rs_r,
):
    zs = inner // 2
    half = zs // 2
    nv, bs = win.shape[1:]
    part = (pl.ds(0, nv // 2), pl.ds(nv // 2, nv // 2))
    pairs = 2 * inner
    total_blocks = rows * inner
    r = lax.axis_index("row")
    i = lax.axis_index("inner")
    z, c = i // 2, lax.rem(i, 2)
    o = 1 - c

    offs = [0]
    for k in range(1, half):
        offs += [-k, k]
    offs.append(half)

    def at_z(step):
        return lax.rem(z + step + zs, zs)

    sibling = (r, 2 * z + o)
    along = ((r, 2 * at_z(1) + c), (r, 2 * at_z(-1) + c))
    beyond = ((r, 2 * at_z(2) + c), (r, 2 * at_z(-2) + c))
    row_up = (lax.rem(r + 1, rows), i)
    row_down = (lax.rem(r + rows - 1, rows), i)
    started = []

    def send(src, dst, s, v, device):
        copy = pltpu.make_async_remote_copy(
            src_ref=src, dst_ref=dst, send_sem=s, recv_sem=v,
            device_id=device, device_id_type=MESH,
        )
        copy.start()
        started.append(copy)
        return copy

    def pos(g, parity, j=0):
        return (g * 2 + parity) * zs + j

    def run(g, parity, span):
        return pl.ds(pos(g, parity, span[0]), span[1])

    loads = []
    for k, (src, dst) in enumerate(
        ((now, win.at[pos(1, c)]), (cotp, v_cotp), (cotd, v_cotd), (h, hbuf), (prev, v_prev), (dens, v_dens))
    ):
        copy = pltpu.make_async_copy(src, dst, in_sem.at[k])
        copy.start()
        loads.append(copy)

    barrier = pltpu.get_barrier_semaphore()
    for device in (sibling, *along, *beyond, row_up, row_down):
        pl.semaphore_signal(barrier, inc=1, device_id=device, device_id_type=MESH)

    scale = coeff[0]
    loads[1].wait()
    loads[2].wait()
    cot[pos(0, c)] = (v_cotp[...].astype(F32) + scale * v_cotd[...].astype(F32)).astype(BF16)
    loads[0].wait()
    pl.semaphore_wait(barrier, 7)

    held = (win, cot)
    base = (1, 0)
    ring = {}
    sib = {}
    ysent = {}
    spans = [(0, 1)] + [(2 * k - 1, 2) for k in range(1, half)] + [(zs - 1, 1)]

    def place(a, j):
        return held[a].at[pos(base[a], c, j)]

    def pass_on(a, way, kind):
        came, goes, device = (
            (0, 3, beyond), (0, 1, along), (3, 5, along), (3, zs - 1, beyond)
        )[kind]
        src = place(a, came + way if came else 0)
        dst = place(a, goes + way if kind < 3 else goes)
        if kind == 3:
            src, dst = src.at[part[way]], dst.at[part[way]]
        ring[a, way, kind] = send(
            src, dst, ring_s.at[a, way, kind], ring_r.at[a, way, kind], device[way]
        )

    def own_out(a, kind):
        for way in range(2):
            pass_on(a, way, kind)

    def came_in(a, kind):
        for way in range(2):
            ring[a, way, kind].wait_recv()
            if kind == 0:
                pass_on(a, way, 2)
                pass_on(a, way, 3)

    def to_sibling(a, n):
        ref = held[a].at[run(base[a], c, spans[n])]
        sib[a, n] = send(ref, ref, sib_s.at[a, n], sib_r.at[a, n], sibling)

    def to_rows(n):
        src = win.at[run(1, c, spans[n])]
        for way, g, device in ((0, 2, row_down), (1, 0, row_up)):
            ysent[way, n] = send(
                src, win.at[run(g, c, spans[n])], y_s.at[way, n], y_r.at[way, n], device
            )

    own_out(1, 0)
    own_out(1, 1)
    to_sibling(1, 0)
    to_rows(0)
    own_out(0, 0)

    def block_of(j, parity):
        return 2 * at_z(offs[j]) + parity

    uses = []
    for n, whose in (
        (0, 0), (0, 1), (2, 0), (2, 1), (1, 0), (1, 1), (3, 0), (4, 0), (3, 1), (4, 1)
    ):
        begin, count = spans[n]
        uses += [(j, whose) for j in range(begin, begin + count)]
    parities = (c, o)

    first = r * inner
    listed = []
    for n, (j, whose) in enumerate(uses):
        b = block_of(j, parities[whose])
        for s in range(2):
            w = lax.rem(cols[s, b] - first + inner + total_blocks, total_blocks)
            w = jnp.minimum(w, 3 * inner - 1)
            g, ii = w // inner, lax.rem(w, inner)
            rel = lax.rem(ii // 2 - z + zs, zs)
            jj = jnp.where(rel <= half, jnp.minimum(2 * rel, zs - 1), 2 * (zs - rel) - 1)
            listed.append(pos(g, lax.rem(ii, 2), jj))
            where[2 * n + s] = listed[-1]

    lane = lax.broadcasted_iota(jnp.int32, (1, 128), 1)
    ends = jnp.full((1, 128), pairs, jnp.int32)
    spots = jnp.full((1, 128), -1, jnp.int32)
    before = jnp.full((1, 128), pairs, jnp.int32)
    for q in range(pairs):
        ends = jnp.where(lane == listed[q], q, ends)
        spots = jnp.where(lane == q, listed[q], spots)
    for q in range(pairs):
        before = jnp.where((spots == listed[q]) & (lane > q), q, before)
    v_links[0:1, :] = ends
    v_links[1:2, :] = before
    links = pltpu.make_async_copy(v_links, link, in_sem.at[6])
    links.start()

    chain[pairs] = jnp.zeros((nv, bs), F32)

    def hcat(b):
        return jnp.concatenate([hbuf[b, 0], hbuf[b, 1]], axis=1)

    def back(n, j, parity):
        got = dot(cot[pos(0, parity, j)], hcat(block_of(j, parity)), NN)
        for s in range(2):
            q = 2 * n + s
            chain[q] = got[:, s * bs : (s + 1) * bs] + chain[link[1, q]]

    def backs(n, whose):
        begin, count = spans[n]
        for j in range(begin, begin + count):
            back(uses.index((j, whose)), j, parities[whose])

    ysib = {}
    packs = ((0, half + 1), (half + 1, half - 1))

    def y_wait(n):
        for way in range(2):
            ysent[way, n].wait_recv()

    def pack_out(m):
        for way, g in ((0, 2), (1, 0)):
            ref = win.at[run(g, c, packs[m])]
            ysib[way, m] = send(ref, ref, ysib_s.at[way, m], ysib_r.at[way, m], sibling)
        ref = win.at[run(1, c, packs[m])]
        ysib[2, m] = send(ref, ref, ysib_s.at[2, m], ysib_r.at[2, m], sibling)

    def backs_there(n):
        sib[1, n].wait_recv()
        backs(n, 1)

    came_in(1, 0)
    to_sibling(1, 2)
    own_out(0, 1)
    loads[3].wait()
    links.wait()
    backs(0, 0)
    backs_there(0)
    came_in(1, 1)
    to_sibling(1, 1)
    backs(2, 0)
    came_in(0, 0)
    to_rows(2)
    backs_there(2)
    backs(1, 0)
    came_in(1, 2)
    to_sibling(1, 3)
    came_in(1, 3)
    to_sibling(1, 4)
    came_in(0, 1)
    to_rows(1)
    backs_there(1)
    backs(3, 0)
    backs(4, 0)
    came_in(0, 2)
    to_rows(3)
    came_in(0, 3)
    to_rows(4)
    backs_there(3)
    backs_there(4)

    def tail(g, parity, j):
        return chain[link[0, pos(g, parity, j)]]

    cuts = ((zs - 3, 3), (zs - 5, 2), (0, zs - 5))
    tsent = {}

    def tails_out(k, g, m):
        begin, count = cuts[m]
        for j in range(begin, begin + count):
            tout[k, j] = tail(g, o, j).astype(BF16)
        span = pl.ds(begin, count)
        tsent[k, m] = send(
            tout.at[k, span], tsib.at[k, span], tsib_s.at[k, m], tsib_r.at[k, m], sibling
        )

    for m in range(3):
        tails_out(0, 0, m)
        tails_out(1, 2, m)

    for n in (0, 2, 1):
        y_wait(n)
    pack_out(0)
    y_wait(3)
    y_wait(4)
    pack_out(1)
    ty = {}

    def to_owners(n):
        begin, count = spans[n]
        for k, g, device in ((0, 0, row_down), (1, 2, row_up)):
            for j in range(begin, begin + count):
                ysend[k, j] = (tail(g, c, j) + tsib[k, j].astype(F32)).astype(BF16)
            span = pl.ds(begin, count)
            ty[k, n] = send(
                ysend.at[k, span], yrecv.at[k, span], ty_s.at[k, n], ty_r.at[k, n], device
            )

    ready = {half: 0, half - 2: 1, half - 3: 2}
    for n in range(half, -1, -1):
        if n in ready:
            tsent[0, ready[n]].wait_recv()
            tsent[1, ready[n]].wait_recv()
        to_owners(n)
    for m in range(3):
        tails_out(2, 1, m)
    for m in range(2):
        for way in range(3):
            ysib[way, m].wait_recv()

    def picked(n):
        return jnp.concatenate([win[where[2 * n]], win[where[2 * n + 1]]], axis=1)

    def product(n, j, parity, k):
        pout[k, j] = dot(picked(n), hcat(block_of(j, parity)), NT).astype(BF16)

    psent = {}
    for m in range(3):
        begin, count = cuts[m]
        for j in range(begin, begin + count):
            product(uses.index((j, 1)), j, o, 1)
        span = pl.ds(begin, count)
        psent[m] = send(pout.at[1, span], psib.at[span], psib_s.at[m], psib_r.at[m], sibling)
    for j in range(zs - 1, -1, -1):
        product(uses.index((j, 0)), j, c, 0)

    def grad_rows(begin, count):
        for n in range(begin, begin + count):
            j, parity = uses[n][0], parities[uses[n][1]]
            b = block_of(j, parity)
            got = 2.0 * dot(cot[pos(0, parity, j)], picked(n), TN)
            for s in range(2):
                o_gh[b, s] = got[:, s * bs : (s + 1) * bs].astype(BF16)

    def product_here(j):
        return pout[0, j].astype(F32) + psib[j].astype(F32)

    def term_here(j):
        return (
            tail(1, c, j) + tsib[2, j].astype(F32)
            + yrecv[0, j].astype(F32) + yrecv[1, j].astype(F32)
        )

    here = (product_here, term_here)
    rs = {}

    def rs_send(a, way, kind, value, device, span=None):
        out, got = rsend.at[a, way, kind], rrecv.at[a, way, kind]
        if span is not None:
            out, got = out.at[span], got.at[span]
        out[...] = value.astype(BF16)
        rs[a, way, kind] = send(
            out, got, rs_s.at[a, way, kind], rs_r.at[a, way, kind], device[way]
        )

    def rs_far(a):
        far = here[a](zs - 1)
        for way in range(2):
            start = way * (nv // 2)
            rs_send(a, way, 1, far[start : start + nv // 2], beyond, part[way])
        for way in range(2):
            rs_send(a, way, 0, here[a](6 - way), along)

    def rs_middle(a):
        for way in range(2):
            value = here[a](4 - way)
            rs[a, way, 1].wait_recv()
            rs[a, way, 0].wait_recv()
            more = rrecv[a, way, 1, part[way], :].astype(F32)
            blank = jnp.zeros_like(more)
            more = jnp.concatenate((more, blank) if way == 0 else (blank, more), axis=0)
            value = value + rrecv[a, way, 0].astype(F32) + more
            rs_send(a, way, 2, value, beyond)

    def rs_near(a):
        for way in range(2):
            rs_send(a, way, 3, here[a](2 - way), along)

    def finish(a):
        value = here[a](0)
        for way in range(2):
            for kind in (3, 2):
                rs[a, way, kind].wait_recv()
                value = value + rrecv[a, way, kind].astype(F32)
        return value

    def y_here(n):
        for k in range(2):
            ty[k, n].wait_recv()

    chunk = inner // 4
    psent[0].wait_recv()
    rs_far(0)
    psent[2].wait_recv()
    rs_near(0)
    grad_rows(0, chunk)
    y_here(4)
    y_here(3)
    tsent[2, 0].wait_recv()
    rs_far(1)
    psent[1].wait_recv()
    rs_middle(0)
    grad_rows(chunk, chunk)
    y_here(2)
    tsent[2, 1].wait_recv()
    rs_middle(1)
    y_here(1)
    tsent[2, 2].wait_recv()
    rs_near(1)
    grad_rows(2 * chunk, 2 * chunk)

    loads[4].wait()
    loads[5].wait()
    nxt = (2.0 * finish(0) - v_prev[...].astype(F32)).astype(BF16)
    o_next[...] = nxt
    o_dens[...] = v_dens[...] + scale * nxt.astype(F32)
    y_here(0)
    o_grad[...] = 2.0 * finish(1)
    for copy in started:
        copy.wait_send()


def write_out(*refs):
    count = len(refs) // 2
    sems = refs[-1]
    copies = [
        pltpu.make_async_copy(refs[k], refs[count + k], sems.at[k]) for k in range(count)
    ]
    for copy in copies:
        copy.start()
    for copy in copies:
        copy.wait()


def per_device(h, cols, now, prev, dens, coeff, cotp, cotd):
    inner, slots, bs, _ = h.shape
    nv = now.shape[1]
    rows = lax.axis_size("row")
    zs, half = inner // 2, inner // 4
    pairs = inner * slots
    blk = (nv, bs)
    any_spec = pl.BlockSpec(memory_space=pl.ANY)
    hbm = pl.BlockSpec(memory_space=pltpu.HBM)
    vmem = pl.BlockSpec(memory_space=pltpu.VMEM)
    smem = pl.BlockSpec(memory_space=pltpu.SMEM)
    vm = pltpu.VMEM
    sem = lambda *shape: pltpu.SemaphoreType.DMA(shape)
    scratch = [
        vm(h.shape, BF16),
        vm(blk, BF16), vm(blk, F32), vm(blk, BF16), vm(blk, BF16),
        vm((3 * inner, *blk), BF16), vm((inner, *blk), BF16), vm((pairs + 1, *blk), F32),
        vm((3, zs, *blk), BF16), vm((3, zs, *blk), BF16),
        vm((2, zs, *blk), BF16), vm((2, zs, *blk), BF16),
        vm((2, zs, *blk), BF16), vm((zs, *blk), BF16),
        vm((2, 2, half, *blk), BF16), vm((2, 2, half, *blk), BF16),
        pltpu.SMEM((pairs,), jnp.int32), pltpu.SMEM((2, 128), jnp.int32),
        vm((2, 128), jnp.int32),
        sem(7), sem(2, 2, 4), sem(2, 2, 4), sem(2, half + 1), sem(2, half + 1),
        sem(2, half + 1), sem(2, half + 1), sem(3, 2), sem(3, 2),
        sem(3, 3), sem(3, 3), sem(2, half + 1), sem(2, half + 1), sem(3), sem(3),
        sem(2, 2, 4), sem(2, 2, 4),
    ]
    out = pl.pallas_call(
        functools.partial(kernel, rows, inner),
        out_shape=(
            jax.ShapeDtypeStruct(blk, BF16),
            jax.ShapeDtypeStruct(blk, F32),
            jax.ShapeDtypeStruct(blk, F32),
            jax.ShapeDtypeStruct(h.shape, BF16),
        ),
        in_specs=[smem, smem] + [hbm] * 6,
        out_specs=(vmem,) * 4,
        scratch_shapes=scratch,
        compiler_params=pltpu.CompilerParams(
            collective_id=0, has_side_effects=True, vmem_limit_bytes=40 * 1024 * 1024
        ),
        cost_estimate=pl.CostEstimate(
            flops=6 * pairs * bs * bs * nv, bytes_accessed=4 * h.size + 20 * bs * nv, transcendentals=0
        ),
    )(pltpu.with_memory_space_constraint(cols.T, pltpu.HBM), coeff, *[pltpu.with_memory_space_constraint(x, pltpu.HBM) for x in (h, now.T, prev.T, dens.T, cotp.T, cotd.T)])
    out = pl.pallas_call(
        write_out,
        out_shape=tuple(jax.ShapeDtypeStruct(x.shape, x.dtype) for x in out),
        in_specs=[any_spec] * 4,
        out_specs=(any_spec,) * 4,
        scratch_shapes=[sem(4)],
        compiler_params=pltpu.CompilerParams(vmem_limit_bytes=1024 * 1024),
    )(*out)
    return (out[0].T, out[1].T, out[2].T, out[3])


def solution(mesh):
    both = P(("row", "inner"), None)
    blocks = P("row", "inner", None, None)
    return jax.shard_map(
        per_device,
        mesh=mesh,
        in_specs=(blocks, P("row", "inner"), both, both, both, P(), both, both),
        out_specs=(both, both, both, blocks),
        check_vma=False,
    )
```

```python
import functools

import jax
import jax.numpy as jnp
from jax import lax
from jax.experimental import pallas as pl
from jax.experimental.pallas import tpu as pltpu
from jax.sharding import PartitionSpec as P

MESH = pl.DeviceIdType.MESH
F32 = jnp.float32
BF16 = jnp.bfloat16
NT = (((1,), (1,)), ((), ()))
NN = (((1,), (0,)), ((), ()))
TN = (((0,), (0,)), ((), ()))


def dot(a, b, dims):
    return lax.dot_general(a, b, dims, preferred_element_type=F32)


def kernel(
    rows, inner, cols, coeff, h, now, prev, dens, cotp, cotd,
    o_next, o_dens, o_grad, o_gh,
    hbuf, v_prev, v_dens, v_cotp, v_cotd,
    win, cot, chain, tout, tsib, ysend, yrecv, pout, psib, rsend, rrecv,
    where, link, v_links,
    in_sem, ring_s, ring_r, sib_s, sib_r, y_s, y_r, ysib_s, ysib_r,
    tsib_s, tsib_r, ty_s, ty_r, psib_s, psib_r, rs_s, rs_r,
):
    zs = inner // 2
    half = zs // 2
    nv, bs = win.shape[1:]
    part = (pl.ds(0, nv // 2), pl.ds(nv // 2, nv // 2))
    pairs = 2 * inner
    total_blocks = rows * inner
    r = lax.axis_index("row")
    i = lax.axis_index("inner")
    z, c = i // 2, lax.rem(i, 2)
    o = 1 - c

    offs = [0]
    for k in range(1, half):
        offs += [-k, k]
    offs.append(half)

    def at_z(step):
        return lax.rem(z + step + zs, zs)

    sibling = (r, 2 * z + o)
    along = ((r, 2 * at_z(1) + c), (r, 2 * at_z(-1) + c))
    beyond = ((r, 2 * at_z(2) + c), (r, 2 * at_z(-2) + c))
    row_up = (lax.rem(r + 1, rows), i)
    row_down = (lax.rem(r + rows - 1, rows), i)
    started = []

    def send(src, dst, s, v, device):
        copy = pltpu.make_async_remote_copy(
            src_ref=src, dst_ref=dst, send_sem=s, recv_sem=v,
            device_id=device, device_id_type=MESH,
        )
        copy.start()
        started.append(copy)
        return copy

    def pos(g, parity, j=0):
        return (g * 2 + parity) * zs + j

    def run(g, parity, span):
        return pl.ds(pos(g, parity, span[0]), span[1])

    loads = []
    for k, (src, dst) in enumerate(
        ((now, win.at[pos(1, c)]), (cotp, v_cotp), (cotd, v_cotd), (h, hbuf), (prev, v_prev), (dens, v_dens))
    ):
        copy = pltpu.make_async_copy(src, dst, in_sem.at[k])
        copy.start()
        loads.append(copy)

    barrier = pltpu.get_barrier_semaphore()
    for device in (sibling, *along, *beyond, row_up, row_down):
        pl.semaphore_signal(barrier, inc=1, device_id=device, device_id_type=MESH)

    scale = coeff[0]
    loads[1].wait()
    loads[2].wait()
    cot[pos(0, c)] = (v_cotp[...].astype(F32) + scale * v_cotd[...].astype(F32)).astype(BF16)
    loads[0].wait()
    pl.semaphore_wait(barrier, 7)

    held = (win, cot)
    base = (1, 0)
    ring = {}
    sib = {}
    ysent = {}
    spans = [(0, 1)] + [(2 * k - 1, 2) for k in range(1, half)] + [(zs - 1, 1)]

    def place(a, j):
        return held[a].at[pos(base[a], c, j)]

    def pass_on(a, way, kind):
        came, goes, device = (
            (0, 3, beyond), (0, 1, along), (3, 5, along), (3, zs - 1, beyond)
        )[kind]
        src = place(a, came + way if came else 0)
        dst = place(a, goes + way if kind < 3 else goes)
        if kind == 3:
            src, dst = src.at[part[way]], dst.at[part[way]]
        ring[a, way, kind] = send(
            src, dst, ring_s.at[a, way, kind], ring_r.at[a, way, kind], device[way]
        )

    def own_out(a, kind):
        for way in range(2):
            pass_on(a, way, kind)

    def came_in(a, kind):
        for way in range(2):
            ring[a, way, kind].wait_recv()
            if kind == 0:
                pass_on(a, way, 2)
                pass_on(a, way, 3)

    def to_sibling(a, n):
        ref = held[a].at[run(base[a], c, spans[n])]
        sib[a, n] = send(ref, ref, sib_s.at[a, n], sib_r.at[a, n], sibling)

    def to_rows(n):
        src = win.at[run(1, c, spans[n])]
        for way, g, device in ((0, 2, row_down), (1, 0, row_up)):
            ysent[way, n] = send(
                src, win.at[run(g, c, spans[n])], y_s.at[way, n], y_r.at[way, n], device
            )

    own_out(1, 0)
    own_out(1, 1)
    to_sibling(1, 0)
    to_rows(0)
    own_out(0, 1)
    own_out(0, 0)

    def block_of(j, parity):
        return 2 * at_z(offs[j]) + parity

    uses = []
    for n, whose in (
        (0, 0), (0, 1), (2, 0), (2, 1), (1, 0), (1, 1), (3, 0), (4, 0), (3, 1), (4, 1)
    ):
        begin, count = spans[n]
        uses += [(j, whose) for j in range(begin, begin + count)]
    parities = (c, o)

    first = r * inner
    listed = []
    for n, (j, whose) in enumerate(uses):
        b = block_of(j, parities[whose])
        for s in range(2):
            w = lax.rem(cols[s, b] - first + inner + total_blocks, total_blocks)
            w = jnp.minimum(w, 3 * inner - 1)
            g, ii = w // inner, lax.rem(w, inner)
            rel = lax.rem(ii // 2 - z + zs, zs)
            jj = jnp.where(rel <= half, jnp.minimum(2 * rel, zs - 1), 2 * (zs - rel) - 1)
            listed.append(pos(g, lax.rem(ii, 2), jj))
            where[2 * n + s] = listed[-1]

    lane = lax.broadcasted_iota(jnp.int32, (1, 128), 1)
    ends = jnp.full((1, 128), pairs, jnp.int32)
    spots = jnp.full((1, 128), -1, jnp.int32)
    before = jnp.full((1, 128), pairs, jnp.int32)
    for q in range(pairs):
        ends = jnp.where(lane == listed[q], q, ends)
        spots = jnp.where(lane == q, listed[q], spots)
    for q in range(pairs):
        before = jnp.where((spots == listed[q]) & (lane > q), q, before)
    v_links[0:1, :] = ends
    v_links[1:2, :] = before
    links = pltpu.make_async_copy(v_links, link, in_sem.at[6])
    links.start()

    chain[pairs] = jnp.zeros((nv, bs), F32)

    def hcat(b):
        return jnp.concatenate([hbuf[b, 0], hbuf[b, 1]], axis=1)

    def back(n, j, parity):
        got = dot(cot[pos(0, parity, j)], hcat(block_of(j, parity)), NN)
        for s in range(2):
            q = 2 * n + s
            chain[q] = got[:, s * bs : (s + 1) * bs] + chain[link[1, q]]

    def backs(n, whose):
        begin, count = spans[n]
        for j in range(begin, begin + count):
            back(uses.index((j, whose)), j, parities[whose])

    ysib = {}
    packs = ((0, half + 1), (half + 1, half - 1))

    def y_wait(n):
        for way in range(2):
            ysent[way, n].wait_recv()

    def pack_out(m):
        for way, g in ((0, 2), (1, 0)):
            ref = win.at[run(g, c, packs[m])]
            ysib[way, m] = send(ref, ref, ysib_s.at[way, m], ysib_r.at[way, m], sibling)
        ref = win.at[run(1, c, packs[m])]
        ysib[2, m] = send(ref, ref, ysib_s.at[2, m], ysib_r.at[2, m], sibling)

    def backs_there(n):
        sib[1, n].wait_recv()
        backs(n, 1)

    came_in(1, 0)
    to_sibling(1, 2)
    loads[3].wait()
    links.wait()
    backs(0, 0)
    backs_there(0)
    came_in(1, 1)
    to_sibling(1, 1)
    backs(2, 0)
    came_in(0, 1)
    to_rows(1)
    came_in(0, 0)
    to_rows(2)
    backs_there(2)
    backs(1, 0)
    came_in(1, 2)
    to_sibling(1, 3)
    came_in(1, 3)
    to_sibling(1, 4)
    backs_there(1)
    backs(3, 0)
    backs(4, 0)
    came_in(0, 2)
    to_rows(3)
    came_in(0, 3)
    to_rows(4)
    backs_there(3)
    backs_there(4)

    def tail(g, parity, j):
        return chain[link[0, pos(g, parity, j)]]

    cuts = ((zs - 3, 3), (zs - 5, 2), (0, zs - 5))
    tsent = {}

    def tails_out(k, g, m):
        begin, count = cuts[m]
        for j in range(begin, begin + count):
            tout[k, j] = tail(g, o, j).astype(BF16)
        span = pl.ds(begin, count)
        tsent[k, m] = send(
            tout.at[k, span], tsib.at[k, span], tsib_s.at[k, m], tsib_r.at[k, m], sibling
        )

    for m in range(3):
        tails_out(0, 0, m)
        tails_out(1, 2, m)

    for n in (0, 2, 1):
        y_wait(n)
    pack_out(0)
    y_wait(3)
    y_wait(4)
    pack_out(1)
    ty = {}

    def to_owners(n):
        begin, count = spans[n]
        for k, g, device in ((0, 0, row_down), (1, 2, row_up)):
            for j in range(begin, begin + count):
                ysend[k, j] = (tail(g, c, j) + tsib[k, j].astype(F32)).astype(BF16)
            span = pl.ds(begin, count)
            ty[k, n] = send(
                ysend.at[k, span], yrecv.at[k, span], ty_s.at[k, n], ty_r.at[k, n], device
            )

    ready = {half: 0, half - 2: 1, half - 3: 2}
    for n in range(half, -1, -1):
        if n in ready:
            tsent[0, ready[n]].wait_recv()
            tsent[1, ready[n]].wait_recv()
        to_owners(n)
    for m in range(3):
        tails_out(2, 1, m)
    for m in range(2):
        for way in range(3):
            ysib[way, m].wait_recv()

    def picked(n):
        return jnp.concatenate([win[where[2 * n]], win[where[2 * n + 1]]], axis=1)

    def product(n, j, parity, k):
        pout[k, j] = dot(picked(n), hcat(block_of(j, parity)), NT).astype(BF16)

    psent = {}
    for m in range(3):
        begin, count = cuts[m]
        for j in range(begin, begin + count):
            product(uses.index((j, 1)), j, o, 1)
        span = pl.ds(begin, count)
        psent[m] = send(pout.at[1, span], psib.at[span], psib_s.at[m], psib_r.at[m], sibling)
    for j in range(zs - 1, -1, -1):
        product(uses.index((j, 0)), j, c, 0)

    def grad_rows(begin, count):
        for n in range(begin, begin + count):
            j, parity = uses[n][0], parities[uses[n][1]]
            b = block_of(j, parity)
            got = 2.0 * dot(cot[pos(0, parity, j)], picked(n), TN)
            for s in range(2):
                o_gh[b, s] = got[:, s * bs : (s + 1) * bs].astype(BF16)

    def product_here(j):
        return pout[0, j].astype(F32) + psib[j].astype(F32)

    def term_here(j):
        return (
            tail(1, c, j) + tsib[2, j].astype(F32)
            + yrecv[0, j].astype(F32) + yrecv[1, j].astype(F32)
        )

    here = (product_here, term_here)
    rs = {}

    def rs_send(a, way, kind, value, device, span=None):
        out, got = rsend.at[a, way, kind], rrecv.at[a, way, kind]
        if span is not None:
            out, got = out.at[span], got.at[span]
        out[...] = value.astype(BF16)
        rs[a, way, kind] = send(
            out, got, rs_s.at[a, way, kind], rs_r.at[a, way, kind], device[way]
        )

    def rs_far(a):
        far = here[a](zs - 1)
        for way in range(2):
            start = way * (nv // 2)
            rs_send(a, way, 1, far[start : start + nv // 2], beyond, part[way])
        for way in range(2):
            rs_send(a, way, 0, here[a](6 - way), along)

    def rs_middle(a):
        for way in range(2):
            value = here[a](4 - way)
            rs[a, way, 1].wait_recv()
            rs[a, way, 0].wait_recv()
            more = rrecv[a, way, 1, part[way], :].astype(F32)
            blank = jnp.zeros_like(more)
            more = jnp.concatenate((more, blank) if way == 0 else (blank, more), axis=0)
            value = value + rrecv[a, way, 0].astype(F32) + more
            rs_send(a, way, 2, value, beyond)

    def rs_near(a):
        for way in range(2):
            rs_send(a, way, 3, here[a](2 - way), along)

    def finish(a):
        value = here[a](0)
        for way in range(2):
            for kind in (3, 2):
                rs[a, way, kind].wait_recv()
                value = value + rrecv[a, way, kind].astype(F32)
        return value

    def y_here(n):
        for k in range(2):
            ty[k, n].wait_recv()

    chunk = inner // 4
    psent[0].wait_recv()
    rs_far(0)
    psent[2].wait_recv()
    rs_near(0)
    grad_rows(0, chunk)
    y_here(4)
    y_here(3)
    tsent[2, 0].wait_recv()
    rs_far(1)
    psent[1].wait_recv()
    rs_middle(0)
    grad_rows(chunk, chunk)
    y_here(2)
    tsent[2, 1].wait_recv()
    rs_middle(1)
    y_here(1)
    tsent[2, 2].wait_recv()
    rs_near(1)
    grad_rows(2 * chunk, 2 * chunk)

    loads[4].wait()
    loads[5].wait()
    nxt = (2.0 * finish(0) - v_prev[...].astype(F32)).astype(BF16)
    o_next[...] = nxt
    o_dens[...] = v_dens[...] + scale * nxt.astype(F32)
    y_here(0)
    o_grad[...] = 2.0 * finish(1)
    for copy in started:
        copy.wait_send()


def write_out(*refs):
    count = len(refs) // 2
    sems = refs[-1]
    copies = [
        pltpu.make_async_copy(refs[k], refs[count + k], sems.at[k]) for k in range(count)
    ]
    for copy in copies:
        copy.start()
    for copy in copies:
        copy.wait()


def per_device(h, cols, now, prev, dens, coeff, cotp, cotd):
    inner, slots, bs, _ = h.shape
    nv = now.shape[1]
    rows = lax.axis_size("row")
    zs, half = inner // 2, inner // 4
    pairs = inner * slots
    blk = (nv, bs)
    any_spec = pl.BlockSpec(memory_space=pl.ANY)
    hbm = pl.BlockSpec(memory_space=pltpu.HBM)
    vmem = pl.BlockSpec(memory_space=pltpu.VMEM)
    smem = pl.BlockSpec(memory_space=pltpu.SMEM)
    vm = pltpu.VMEM
    sem = lambda *shape: pltpu.SemaphoreType.DMA(shape)
    scratch = [
        vm(h.shape, BF16),
        vm(blk, BF16), vm(blk, F32), vm(blk, BF16), vm(blk, BF16),
        vm((3 * inner, *blk), BF16), vm((inner, *blk), BF16), vm((pairs + 1, *blk), F32),
        vm((3, zs, *blk), BF16), vm((3, zs, *blk), BF16),
        vm((2, zs, *blk), BF16), vm((2, zs, *blk), BF16),
        vm((2, zs, *blk), BF16), vm((zs, *blk), BF16),
        vm((2, 2, half, *blk), BF16), vm((2, 2, half, *blk), BF16),
        pltpu.SMEM((pairs,), jnp.int32), pltpu.SMEM((2, 128), jnp.int32),
        vm((2, 128), jnp.int32),
        sem(7), sem(2, 2, 4), sem(2, 2, 4), sem(2, half + 1), sem(2, half + 1),
        sem(2, half + 1), sem(2, half + 1), sem(3, 2), sem(3, 2),
        sem(3, 3), sem(3, 3), sem(2, half + 1), sem(2, half + 1), sem(3), sem(3),
        sem(2, 2, 4), sem(2, 2, 4),
    ]
    out = pl.pallas_call(
        functools.partial(kernel, rows, inner),
        out_shape=(
            jax.ShapeDtypeStruct(blk, BF16),
            jax.ShapeDtypeStruct(blk, F32),
            jax.ShapeDtypeStruct(blk, F32),
            jax.ShapeDtypeStruct(h.shape, BF16),
        ),
        in_specs=[smem, smem] + [hbm] * 6,
        out_specs=(vmem,) * 4,
        scratch_shapes=scratch,
        compiler_params=pltpu.CompilerParams(
            collective_id=0, has_side_effects=True, vmem_limit_bytes=40 * 1024 * 1024
        ),
        cost_estimate=pl.CostEstimate(
            flops=6 * pairs * bs * bs * nv, bytes_accessed=4 * h.size + 20 * bs * nv, transcendentals=0
        ),
    )(pltpu.with_memory_space_constraint(cols.T, pltpu.HBM), coeff, *[pltpu.with_memory_space_constraint(x, pltpu.HBM) for x in (h, now.T, prev.T, dens.T, cotp.T, cotd.T)])
    out = pl.pallas_call(
        write_out,
        out_shape=tuple(jax.ShapeDtypeStruct(x.shape, x.dtype) for x in out),
        in_specs=[any_spec] * 4,
        out_specs=(any_spec,) * 4,
        scratch_shapes=[sem(4)],
        compiler_params=pltpu.CompilerParams(vmem_limit_bytes=1024 * 1024),
    )(*out)
    return (out[0].T, out[1].T, out[2].T, out[3])


def solution(mesh):
    both = P(("row", "inner"), None)
    blocks = P("row", "inner", None, None)
    return jax.shard_map(
        per_device,
        mesh=mesh,
        in_specs=(blocks, P("row", "inner"), both, both, both, P(), both, both),
        out_specs=(both, both, both, blocks),
        check_vma=False,
    )
```

```python
import functools

import jax
import jax.numpy as jnp
from jax import lax
from jax.experimental import pallas as pl
from jax.experimental.pallas import tpu as pltpu
from jax.sharding import PartitionSpec as P

MESH = pl.DeviceIdType.MESH
F32 = jnp.float32
BF16 = jnp.bfloat16
NT = (((1,), (1,)), ((), ()))
NN = (((1,), (0,)), ((), ()))
TN = (((0,), (0,)), ((), ()))


def dot(a, b, dims):
    return lax.dot_general(a, b, dims, preferred_element_type=F32)


def kernel(
    rows, inner, cols, coeff, h, now, prev, dens, cotp, cotd,
    o_next, o_dens, o_grad, o_gh,
    hbuf, v_prev, v_dens, v_cotp, v_cotd,
    win, cot, chain, tout, tsib, ysend, yrecv, pout, psib, rsend, rrecv,
    where, link, v_links,
    in_sem, ring_s, ring_r, sib_s, sib_r, y_s, y_r, ysib_s, ysib_r,
    tsib_s, tsib_r, ty_s, ty_r, psib_s, psib_r, rs_s, rs_r,
):
    zs = inner // 2
    half = zs // 2
    nv, bs = win.shape[1:]
    part = (pl.ds(0, nv // 2), pl.ds(nv // 2, nv // 2))
    pairs = 2 * inner
    total_blocks = rows * inner
    r = lax.axis_index("row")
    i = lax.axis_index("inner")
    z, c = i // 2, lax.rem(i, 2)
    o = 1 - c

    offs = [0]
    for k in range(1, half):
        offs += [-k, k]
    offs.append(half)

    def at_z(step):
        return lax.rem(z + step + zs, zs)

    sibling = (r, 2 * z + o)
    along = ((r, 2 * at_z(1) + c), (r, 2 * at_z(-1) + c))
    beyond = ((r, 2 * at_z(2) + c), (r, 2 * at_z(-2) + c))
    row_up = (lax.rem(r + 1, rows), i)
    row_down = (lax.rem(r + rows - 1, rows), i)
    started = []

    def send(src, dst, s, v, device):
        copy = pltpu.make_async_remote_copy(
            src_ref=src, dst_ref=dst, send_sem=s, recv_sem=v,
            device_id=device, device_id_type=MESH,
        )
        copy.start()
        started.append(copy)
        return copy

    def pos(g, parity, j=0):
        return (g * 2 + parity) * zs + j

    def run(g, parity, span):
        return pl.ds(pos(g, parity, span[0]), span[1])

    loads = []
    for k, (src, dst) in enumerate(
        ((now, win.at[pos(1, c)]), (cotp, v_cotp), (cotd, v_cotd), (h, hbuf), (prev, v_prev), (dens, v_dens))
    ):
        copy = pltpu.make_async_copy(src, dst, in_sem.at[k])
        copy.start()
        loads.append(copy)

    barrier = pltpu.get_barrier_semaphore()
    for device in (sibling, *along, *beyond, row_up, row_down):
        pl.semaphore_signal(barrier, inc=1, device_id=device, device_id_type=MESH)

    scale = coeff[0]
    loads[1].wait()
    loads[2].wait()
    cot[pos(0, c)] = (v_cotp[...].astype(F32) + scale * v_cotd[...].astype(F32)).astype(BF16)
    loads[0].wait()
    pl.semaphore_wait(barrier, 7)

    held = (win, cot)
    base = (1, 0)
    ring = {}
    sib = {}
    ysent = {}
    spans = [(0, 1)] + [(2 * k - 1, 2) for k in range(1, half)] + [(zs - 1, 1)]

    def place(a, j):
        return held[a].at[pos(base[a], c, j)]

    def pass_on(a, way, kind):
        came, goes, device = (
            (0, 3, beyond), (0, 1, along), (3, 5, along), (3, zs - 1, beyond)
        )[kind]
        src = place(a, came + way if came else 0)
        dst = place(a, goes + way if kind < 3 else goes)
        if kind == 3:
            src, dst = src.at[part[way]], dst.at[part[way]]
        ring[a, way, kind] = send(
            src, dst, ring_s.at[a, way, kind], ring_r.at[a, way, kind], device[way]
        )

    def own_out(a, kind):
        for way in range(2):
            pass_on(a, way, kind)

    def came_in(a, kind):
        for way in range(2):
            ring[a, way, kind].wait_recv()
            if kind == 0:
                pass_on(a, way, 2)
                pass_on(a, way, 3)

    def to_sibling(a, n):
        ref = held[a].at[run(base[a], c, spans[n])]
        sib[a, n] = send(ref, ref, sib_s.at[a, n], sib_r.at[a, n], sibling)

    def to_rows(n):
        src = win.at[run(1, c, spans[n])]
        for way, g, device in ((0, 2, row_down), (1, 0, row_up)):
            ysent[way, n] = send(
                src, win.at[run(g, c, spans[n])], y_s.at[way, n], y_r.at[way, n], device
            )

    to_rows(0)
    own_out(1, 0)
    own_out(1, 1)
    to_sibling(1, 0)
    own_out(0, 1)
    own_out(0, 0)

    def block_of(j, parity):
        return 2 * at_z(offs[j]) + parity

    uses = []
    for n, whose in (
        (0, 0), (0, 1), (2, 0), (2, 1), (1, 0), (1, 1), (3, 0), (4, 0), (3, 1), (4, 1)
    ):
        begin, count = spans[n]
        uses += [(j, whose) for j in range(begin, begin + count)]
    parities = (c, o)

    first = r * inner
    listed = []
    for n, (j, whose) in enumerate(uses):
        b = block_of(j, parities[whose])
        for s in range(2):
            w = lax.rem(cols[s, b] - first + inner + total_blocks, total_blocks)
            w = jnp.minimum(w, 3 * inner - 1)
            g, ii = w // inner, lax.rem(w, inner)
            rel = lax.rem(ii // 2 - z + zs, zs)
            jj = jnp.where(rel <= half, jnp.minimum(2 * rel, zs - 1), 2 * (zs - rel) - 1)
            listed.append(pos(g, lax.rem(ii, 2), jj))
            where[2 * n + s] = listed[-1]

    lane = lax.broadcasted_iota(jnp.int32, (1, 128), 1)
    ends = jnp.full((1, 128), pairs, jnp.int32)
    spots = jnp.full((1, 128), -1, jnp.int32)
    before = jnp.full((1, 128), pairs, jnp.int32)
    for q in range(pairs):
        ends = jnp.where(lane == listed[q], q, ends)
        spots = jnp.where(lane == q, listed[q], spots)
    for q in range(pairs):
        before = jnp.where((spots == listed[q]) & (lane > q), q, before)
    v_links[0:1, :] = ends
    v_links[1:2, :] = before
    links = pltpu.make_async_copy(v_links, link, in_sem.at[6])
    links.start()

    chain[pairs] = jnp.zeros((nv, bs), F32)

    def hcat(b):
        return jnp.concatenate([hbuf[b, 0], hbuf[b, 1]], axis=1)

    def back(n, j, parity):
        got = dot(cot[pos(0, parity, j)], hcat(block_of(j, parity)), NN)
        for s in range(2):
            q = 2 * n + s
            chain[q] = got[:, s * bs : (s + 1) * bs] + chain[link[1, q]]

    def backs(n, whose):
        begin, count = spans[n]
        for j in range(begin, begin + count):
            back(uses.index((j, whose)), j, parities[whose])

    ysib = {}
    packs = ((0, half + 1), (half + 1, half - 1))

    def y_wait(n):
        for way in range(2):
            ysent[way, n].wait_recv()

    def pack_out(m):
        for way, g in ((0, 2), (1, 0)):
            ref = win.at[run(g, c, packs[m])]
            ysib[way, m] = send(ref, ref, ysib_s.at[way, m], ysib_r.at[way, m], sibling)
        ref = win.at[run(1, c, packs[m])]
        ysib[2, m] = send(ref, ref, ysib_s.at[2, m], ysib_r.at[2, m], sibling)

    def backs_there(n):
        sib[1, n].wait_recv()
        backs(n, 1)

    came_in(1, 0)
    to_sibling(1, 2)
    loads[3].wait()
    links.wait()
    backs(0, 0)
    backs_there(0)
    came_in(1, 1)
    to_sibling(1, 1)
    backs(2, 0)
    came_in(0, 1)
    to_rows(1)
    came_in(0, 0)
    to_rows(2)
    backs_there(2)
    backs(1, 0)
    came_in(1, 2)
    to_sibling(1, 3)
    came_in(1, 3)
    to_sibling(1, 4)
    backs_there(1)
    backs(3, 0)
    backs(4, 0)
    came_in(0, 2)
    to_rows(3)
    came_in(0, 3)
    to_rows(4)
    backs_there(3)
    backs_there(4)

    def tail(g, parity, j):
        return chain[link[0, pos(g, parity, j)]]

    cuts = ((zs - 3, 3), (zs - 5, 2), (0, zs - 5))
    tsent = {}

    def tails_out(k, g, m):
        begin, count = cuts[m]
        for j in range(begin, begin + count):
            tout[k, j] = tail(g, o, j).astype(BF16)
        span = pl.ds(begin, count)
        tsent[k, m] = send(
            tout.at[k, span], tsib.at[k, span], tsib_s.at[k, m], tsib_r.at[k, m], sibling
        )

    for m in range(3):
        tails_out(0, 0, m)
        tails_out(1, 2, m)

    for n in (0, 2, 1):
        y_wait(n)
    pack_out(0)
    y_wait(3)
    y_wait(4)
    pack_out(1)
    ty = {}

    def to_owners(n):
        begin, count = spans[n]
        for k, g, device in ((0, 0, row_down), (1, 2, row_up)):
            for j in range(begin, begin + count):
                ysend[k, j] = (tail(g, c, j) + tsib[k, j].astype(F32)).astype(BF16)
            span = pl.ds(begin, count)
            ty[k, n] = send(
                ysend.at[k, span], yrecv.at[k, span], ty_s.at[k, n], ty_r.at[k, n], device
            )

    ready = {half: 0, half - 2: 1, half - 3: 2}
    for n in range(half, -1, -1):
        if n in ready:
            tsent[0, ready[n]].wait_recv()
            tsent[1, ready[n]].wait_recv()
        to_owners(n)
    for m in range(3):
        tails_out(2, 1, m)
    for m in range(2):
        for way in range(3):
            ysib[way, m].wait_recv()

    def picked(n):
        return jnp.concatenate([win[where[2 * n]], win[where[2 * n + 1]]], axis=1)

    def product(n, j, parity, k):
        pout[k, j] = dot(picked(n), hcat(block_of(j, parity)), NT).astype(BF16)

    psent = {}
    for m in range(3):
        begin, count = cuts[m]
        for j in range(begin, begin + count):
            product(uses.index((j, 1)), j, o, 1)
        span = pl.ds(begin, count)
        psent[m] = send(pout.at[1, span], psib.at[span], psib_s.at[m], psib_r.at[m], sibling)
    for j in range(zs - 1, -1, -1):
        product(uses.index((j, 0)), j, c, 0)

    def grad_rows(begin, count):
        for n in range(begin, begin + count):
            j, parity = uses[n][0], parities[uses[n][1]]
            b = block_of(j, parity)
            got = 2.0 * dot(cot[pos(0, parity, j)], picked(n), TN)
            for s in range(2):
                o_gh[b, s] = got[:, s * bs : (s + 1) * bs].astype(BF16)

    def product_here(j):
        return pout[0, j].astype(F32) + psib[j].astype(F32)

    def term_here(j):
        return (
            tail(1, c, j) + tsib[2, j].astype(F32)
            + yrecv[0, j].astype(F32) + yrecv[1, j].astype(F32)
        )

    here = (product_here, term_here)
    rs = {}

    def rs_send(a, way, kind, value, device, span=None):
        out, got = rsend.at[a, way, kind], rrecv.at[a, way, kind]
        if span is not None:
            out, got = out.at[span], got.at[span]
        out[...] = value.astype(BF16)
        rs[a, way, kind] = send(
            out, got, rs_s.at[a, way, kind], rs_r.at[a, way, kind], device[way]
        )

    def rs_far(a):
        far = here[a](zs - 1)
        for way in range(2):
            start = way * (nv // 2)
            rs_send(a, way, 1, far[start : start + nv // 2], beyond, part[way])
        for way in range(2):
            rs_send(a, way, 0, here[a](6 - way), along)

    def rs_middle(a):
        for way in range(2):
            value = here[a](4 - way)
            rs[a, way, 1].wait_recv()
            rs[a, way, 0].wait_recv()
            more = rrecv[a, way, 1, part[way], :].astype(F32)
            blank = jnp.zeros_like(more)
            more = jnp.concatenate((more, blank) if way == 0 else (blank, more), axis=0)
            value = value + rrecv[a, way, 0].astype(F32) + more
            rs_send(a, way, 2, value, beyond)

    def rs_near(a):
        for way in range(2):
            rs_send(a, way, 3, here[a](2 - way), along)

    def finish(a):
        value = here[a](0)
        for way in range(2):
            for kind in (3, 2):
                rs[a, way, kind].wait_recv()
                value = value + rrecv[a, way, kind].astype(F32)
        return value

    def y_here(n):
        for k in range(2):
            ty[k, n].wait_recv()

    chunk = inner // 4
    psent[0].wait_recv()
    rs_far(0)
    psent[2].wait_recv()
    rs_near(0)
    y_here(4)
    y_here(3)
    tsent[2, 0].wait_recv()
    rs_far(1)
    grad_rows(0, chunk)
    psent[1].wait_recv()
    rs_middle(0)
    grad_rows(chunk, chunk)
    y_here(2)
    tsent[2, 1].wait_recv()
    rs_middle(1)
    y_here(1)
    tsent[2, 2].wait_recv()
    rs_near(1)
    grad_rows(2 * chunk, 2 * chunk)

    loads[4].wait()
    loads[5].wait()
    nxt = (2.0 * finish(0) - v_prev[...].astype(F32)).astype(BF16)
    o_next[...] = nxt
    o_dens[...] = v_dens[...] + scale * nxt.astype(F32)
    y_here(0)
    o_grad[...] = 2.0 * finish(1)
    for copy in started:
        copy.wait_send()


def write_out(*refs):
    count = len(refs) // 2
    sems = refs[-1]
    copies = [
        pltpu.make_async_copy(refs[k], refs[count + k], sems.at[k]) for k in range(count)
    ]
    for copy in copies:
        copy.start()
    for copy in copies:
        copy.wait()


def per_device(h, cols, now, prev, dens, coeff, cotp, cotd):
    inner, slots, bs, _ = h.shape
    nv = now.shape[1]
    rows = lax.axis_size("row")
    zs, half = inner // 2, inner // 4
    pairs = inner * slots
    blk = (nv, bs)
    any_spec = pl.BlockSpec(memory_space=pl.ANY)
    hbm = pl.BlockSpec(memory_space=pltpu.HBM)
    vmem = pl.BlockSpec(memory_space=pltpu.VMEM)
    smem = pl.BlockSpec(memory_space=pltpu.SMEM)
    vm = pltpu.VMEM
    sem = lambda *shape: pltpu.SemaphoreType.DMA(shape)
    scratch = [
        vm(h.shape, BF16),
        vm(blk, BF16), vm(blk, F32), vm(blk, BF16), vm(blk, BF16),
        vm((3 * inner, *blk), BF16), vm((inner, *blk), BF16), vm((pairs + 1, *blk), F32),
        vm((3, zs, *blk), BF16), vm((3, zs, *blk), BF16),
        vm((2, zs, *blk), BF16), vm((2, zs, *blk), BF16),
        vm((2, zs, *blk), BF16), vm((zs, *blk), BF16),
        vm((2, 2, half, *blk), BF16), vm((2, 2, half, *blk), BF16),
        pltpu.SMEM((pairs,), jnp.int32), pltpu.SMEM((2, 128), jnp.int32),
        vm((2, 128), jnp.int32),
        sem(7), sem(2, 2, 4), sem(2, 2, 4), sem(2, half + 1), sem(2, half + 1),
        sem(2, half + 1), sem(2, half + 1), sem(3, 2), sem(3, 2),
        sem(3, 3), sem(3, 3), sem(2, half + 1), sem(2, half + 1), sem(3), sem(3),
        sem(2, 2, 4), sem(2, 2, 4),
    ]
    out = pl.pallas_call(
        functools.partial(kernel, rows, inner),
        out_shape=(
            jax.ShapeDtypeStruct(blk, BF16),
            jax.ShapeDtypeStruct(blk, F32),
            jax.ShapeDtypeStruct(blk, F32),
            jax.ShapeDtypeStruct(h.shape, BF16),
        ),
        in_specs=[smem, smem] + [hbm] * 6,
        out_specs=(vmem,) * 4,
        scratch_shapes=scratch,
        compiler_params=pltpu.CompilerParams(
            collective_id=0, has_side_effects=True, vmem_limit_bytes=40 * 1024 * 1024
        ),
        cost_estimate=pl.CostEstimate(
            flops=6 * pairs * bs * bs * nv, bytes_accessed=4 * h.size + 20 * bs * nv, transcendentals=0
        ),
    )(pltpu.with_memory_space_constraint(cols.T, pltpu.HBM), coeff, *[pltpu.with_memory_space_constraint(x, pltpu.HBM) for x in (h, now.T, prev.T, dens.T, cotp.T, cotd.T)])
    out = pl.pallas_call(
        write_out,
        out_shape=tuple(jax.ShapeDtypeStruct(x.shape, x.dtype) for x in out),
        in_specs=[any_spec] * 4,
        out_specs=(any_spec,) * 4,
        scratch_shapes=[sem(4)],
        compiler_params=pltpu.CompilerParams(vmem_limit_bytes=1024 * 1024),
    )(*out)
    return (out[0].T, out[1].T, out[2].T, out[3])


def solution(mesh):
    both = P(("row", "inner"), None)
    blocks = P("row", "inner", None, None)
    return jax.shard_map(
        per_device,
        mesh=mesh,
        in_specs=(blocks, P("row", "inner"), both, both, both, P(), both, both),
        out_specs=(both, both, both, blocks),
        check_vma=False,
    )
```
